256 devices in a mesh: section: 8 (over y, x_lo), ts: 32 (over z, x_hi, core).
Axes of the slice: x: 4 (x_hi: 2, x_lo: 2; x = x_hi * 2 + x_lo), y: 4, z: 8, core: 2. Of those that a mesh axis runs over, the one named last changes fastest.
Arguments:
- upstream: bfloat16 [8, 4096, 8192], P('section', None, 'ts'), as said below
- stashed: bfloat16 [8, 4096, 8192], P('section', None, 'ts'), as said below
- returning: bfloat16 [8, 4096, 8192], P('section', None, 'ts'), may hold values from -3 to 3
- key_cotangent: bfloat16 [8, 4096, 1024], P('section', 'ts'), as said below
- key_weight: bfloat16 [8, 8192, 1024], P('section', 'ts'), as said below
- norm_gain: float32 [8, 8192], P('section', 'ts'), may hold values from 0.1 to 1.9
- lengths: int32 [8], P('section'), may hold values from 512 to 4096, as said below
Outputs:
- new_keys: bfloat16 [8, 4096, 1024], P('section', 'ts')
- input_grad: bfloat16 [8, 4096, 8192], P('section', None, 'ts')
- weight_grad: float32 [8, 8192, 1024], P('section', 'ts')
- gain_grad: float32 [8, 8192], P('section', 'ts')
The draws below stay inside these ranges and needn't reach their ends.
Inputs may be any that keep to these rules, and one draw needn't show every extreme that they name: `lengths`: some section has all 4096 tokens live in every draw. `upstream`: float entries; every token row has positive mean square. `stashed`: float entries; every token row has positive mean square. `key_cotangent`: float entries. `key_weight`: float entries.
All inputs are finite; a program needn't handle non-finite values.
Results may differ from the reference program's by a relative error of at most 0.023.
Values may be sent and summed in bfloat16 or wider, within the bound.
No kernel may reach another device: no remote copies, remote signals or barrier semaphores. Data moves between devices by JAX's collectives and lax.ppermute only.
A program may use at most 128 MiB of HBM per device.

```python
import math
import jax
import jax.numpy as jnp
from jax import lax

D = 8192
F = 1024
TOKENS = 4096
N_SECTION = 8
N_TS = 32


def coupling(key):
    key = jax.random.fold_in(key, 5)
    first, second, third = jax.random.split(key, 3)
    signs = jnp.where(jax.random.randint(first, (D,), 0, 2, jnp.int32) == 1, 1.0, -1.0).astype(jnp.float32)
    paired = (jax.random.permutation(second, D) % F).astype(jnp.int32)
    direction = jax.random.normal(third, (F,), jnp.float32)
    return (signs, paired, direction)


def stream_field(key, shared_rows):
    first = jax.random.fold_in(key, 0)
    second = jax.random.fold_in(key, 1)
    fourth = jax.random.fold_in(key, 3)
    rows = jnp.exp(jax.random.uniform(second, (N_SECTION, TOKENS, 1), jnp.float32) * math.log(10.0))
    columns = jnp.exp(math.log(3.0) * jnp.arange(D, dtype=jnp.float32) / D)
    base = jax.random.normal(first, (N_SECTION, TOKENS, D), jnp.float32)
    base = base + shared_rows
    loud_block = jax.random.randint(fourth, (N_SECTION, TOKENS, 1), 0, N_TS, jnp.int32)
    feature_block = (jnp.arange(D, dtype=jnp.int32) // (D // N_TS)).astype(jnp.int32)
    loudness = jnp.where(feature_block[None, None, :] == loud_block, 8.0, 1.0).astype(jnp.float32)
    return jnp.clip(base * rows * columns * 0.5, -15.0, 15.0) * loudness


def draw_upstream(key, part):
    key = jax.random.fold_in(key, 11)
    return stream_field(key, jnp.zeros((1, 1, D), jnp.float32)).astype(jnp.bfloat16)


def draw_stashed(key, part):
    signs, paired, direction = coupling(key)
    key = jax.random.fold_in(key, 23)
    sign_key = jax.random.fold_in(key, 7)
    token_signs = jnp.where(jax.random.randint(sign_key, (N_SECTION, TOKENS, 1), 0, 2, jnp.int32) == 1, 1.0, -1.0).astype(jnp.float32)
    shared_row = signs * jnp.take(direction, paired)
    return stream_field(key, token_signs * shared_row[None, None, :]).astype(jnp.bfloat16)


def draw_key_weight(key, part):
    signs, paired, direction = coupling(key)
    key = jax.random.fold_in(key, 41)
    noise = jax.random.normal(key, (N_SECTION, D, F), jnp.float32)
    chosen = (paired[:, None] == jnp.arange(F, dtype=jnp.int32)[None, :]).astype(jnp.float32)
    sparse = chosen * signs[:, None] * math.sqrt(F / D)
    return (noise * (1.0 / math.sqrt(D)) + sparse[None, :, :]).astype(jnp.bfloat16)


def draw_key_cotangent(key, part):
    signs, paired, direction = coupling(key)
    key = jax.random.fold_in(key, 53)
    first, second = jax.random.split(key)
    strength = jax.random.normal(first, (N_SECTION, TOKENS, 1), jnp.float32)
    noise = jax.random.normal(second, (N_SECTION, TOKENS, F), jnp.float32)
    return jnp.clip(strength * direction[None, None, :] + noise, -8.0, 8.0).astype(jnp.bfloat16)


def draw_lengths(key, part):
    key = jax.random.fold_in(key, 37)
    first, second = jax.random.split(key)
    values = jax.random.randint(first, (N_SECTION,), TOKENS // 8, TOKENS + 1, jnp.int32)
    fullest = jax.random.randint(second, (), 0, N_SECTION, jnp.int32)
    return jnp.where(jnp.arange(N_SECTION, dtype=jnp.int32) == fullest, TOKENS, values).astype(jnp.int32)


def steps_of(key, dims, pieces, smallest, high):
    level, own = 1.0, jax.random.fold_in(key, 6)
    for axis_at, shards_of in pieces:
        steps = jnp.exp(jax.random.uniform(jax.random.fold_in(own, axis_at), (shards_of,), jnp.float32, smallest / len(pieces), high / len(pieces)))
        level = level * jnp.repeat(steps, dims[axis_at] // shards_of).reshape([-1 if axis == axis_at else 1 for axis in range(len(dims))])
    return level


def normal_values(own_key, shape, scale, most, pieces=(), held_as=jnp.bfloat16):
    array = scale * jax.random.normal(own_key, shape, jnp.float32)
    if pieces:
        array = array * steps_of(own_key, shape, pieces, -0.22, 0.18)
    return jnp.clip(array, -most, most).astype(held_as)


def setup_inputs(seed: int = 0) -> dict:
    streams_of = jax.random.split(jax.random.key(seed), 8)
    return {
        "upstream": draw_upstream(jax.random.fold_in(streams_of[7], 71), 0),
        "stashed": draw_stashed(jax.random.fold_in(streams_of[7], 71), 0),
        "returning": normal_values(streams_of[2], (N_SECTION, TOKENS, D), 0.3, 3.0, ((0, 8), (2, 32))),
        "key_cotangent": draw_key_cotangent(jax.random.fold_in(streams_of[7], 71), 0),
        "key_weight": draw_key_weight(jax.random.fold_in(streams_of[7], 71), 0),
        "norm_gain": jnp.clip(1.0 + 0.18 * jax.random.normal(streams_of[5], (N_SECTION, D), jnp.float32), 0.1, 1.9),
        "lengths": draw_lengths(jax.random.fold_in(streams_of[7], 71), 0),
    }


eps = 1e-05

def row_rate(block):
    wide = block.astype(jnp.float32)
    return lax.rsqrt(lax.optimization_barrier(jnp.sum(wide * wide, axis=1)) / D + eps)

def reference(upstream, stashed, returning, key_cotangent, key_weight, norm_gain, lengths):
    width_block = D // N_TS
    keys_all = []
    grads_all = []
    weights_all = []
    gains_all = []
    for section_id in range(N_SECTION):
        inbound = upstream[(section_id - 1) % N_SECTION]
        downstream = returning[(section_id + 1) % N_SECTION]
        older = stashed[N_SECTION - 1 - section_id]
        weights = key_weight[section_id]
        gain_row = norm_gain[section_id]
        fresh_rate = row_rate(inbound)
        older_rate = row_rate(older)
        scaled = (inbound.astype(jnp.float32) * gain_row).astype(jnp.bfloat16)
        older_scaled = (older.astype(jnp.float32) * gain_row).astype(jnp.bfloat16)

        def block_term(total, index):
            cols = lax.dynamic_slice_in_dim(scaled, index * width_block, width_block, 1)
            rows = lax.dynamic_slice_in_dim(weights, index * width_block, width_block, 0)
            part = jnp.dot(cols, rows, preferred_element_type=jnp.float32)
            return (total + part.astype(jnp.bfloat16).astype(jnp.float32), None)
        partial_keys, _ = lax.scan(block_term, jnp.zeros((TOKENS, F), jnp.float32), jnp.arange(N_TS, dtype=jnp.int32))
        keys_all.append((partial_keys * fresh_rate[:, None]).astype(jnp.bfloat16))
        positions = jnp.arange(TOKENS, dtype=jnp.int32)
        live = (positions < lengths[section_id]).astype(jnp.float32)
        graded = (key_cotangent[section_id].astype(jnp.float32) * (live * older_rate)[:, None]).astype(jnp.bfloat16)
        weights_all.append(lax.dot_general(older_scaled, graded, (((0,), (0,)), ((), ())), preferred_element_type=jnp.float32))
        scaled_grad = lax.dot_general(graded, weights, (((1,), (1,)), ((), ())), preferred_element_type=jnp.float32)
        curvature = lax.optimization_barrier(jnp.sum(scaled_grad * older_scaled.astype(jnp.float32), axis=1))
        older_wide = older.astype(jnp.float32)
        total = downstream.astype(jnp.float32) + gain_row * scaled_grad - (older_rate * older_rate / D * curvature)[:, None] * older_wide
        grads_all.append(total.astype(jnp.bfloat16))
        gains_all.append(lax.optimization_barrier(jnp.sum(scaled_grad * older_wide, axis=0)))
    return (jnp.stack(keys_all), jnp.stack(grads_all), jnp.stack(weights_all), jnp.stack(gains_all))
```

```python
import jax
import jax.numpy as jnp
from jax import lax
from jax.experimental import pallas as pl
from jax.experimental.pallas import tpu as pltpu
from jax.sharding import PartitionSpec as P

eps = 1e-05
BF = jnp.bfloat16
F32 = jnp.float32
N_S = 8
N_T = 32
N_Z = 8
TOK = 4096
OWN = TOK // N_T
WIDTH = 8192
LANE = WIDTH // N_T
KEYS = 1024
Z_STEP = 4
PACK = LANE + 16
AXES = ("section", "ts")


def move(value, target, cores=(0, 1)):
    pairs = []
    for s in range(N_S):
        for t in [t for t in range(N_T) if t % 2 in cores]:
            to_s, to_t = target(s, t)
            pairs.append((s * N_T + t, to_s * N_T + to_t))
    return lax.ppermute(value, AXES, pairs)


def to_next(s, t):
    return (s + 1) % N_S, t


def to_previous(s, t):
    return (s - 1) % N_S, t


def to_mirror(s, t):
    return N_S - 1 - s, t


def to_other_core(s, t):
    return s, t ^ 1


def to_other_half(s, t):
    return s, t ^ 2


def to_next_other_half(s, t):
    return (s + 1) % N_S, t ^ 2


def z_up(s, t):
    return s, (t + 4) % N_T


def z_down(s, t):
    return s, (t - 4) % N_T


def pick(value, index):
    return lax.dynamic_index_in_dim(value, index, 0, keepdims=False)


def after(value, *others):
    return lax.optimization_barrier((value,) + others)[0]


def add(a, b):
    return (a.astype(F32) + b.astype(F32)).astype(BF)


def call(kernel, grid, in_specs, out_specs, out_shape, flops, size, aliases=None):
    return pl.pallas_call(
        kernel,
        grid_spec=pltpu.PrefetchScalarGridSpec(
            num_scalar_prefetch=1, grid=grid, in_specs=in_specs, out_specs=out_specs
        ),
        out_shape=out_shape,
        input_output_aliases=aliases or {},
        compiler_params=pltpu.CompilerParams(vmem_limit_bytes=56 * 1024 * 1024),
        cost_estimate=pl.CostEstimate(flops=flops, bytes_accessed=size, transcendentals=0),
    )


def pack_kernel(place, weights, gain, out):
    out[:LANE, :] = weights[...]
    value = gain[...]
    high = value.astype(BF)
    middle = (value - high.astype(F32)).astype(BF)
    low = (value - high.astype(F32) - middle.astype(F32)).astype(BF)
    row = jnp.concatenate([high, middle, low, jnp.zeros((1, LANE), BF)], axis=1)
    out[LANE:, :] = jnp.broadcast_to(row, (PACK - LANE, KEYS))


def pack(place, weights, gain):
    return call(
        pack_kernel,
        (1,),
        [
            pl.BlockSpec((LANE, KEYS), lambda i, place: (0, 0)),
            pl.BlockSpec((1, LANE), lambda i, place: (0, 0)),
        ],
        pl.BlockSpec((PACK, KEYS), lambda i, place: (0, 0)),
        jax.ShapeDtypeStruct((PACK, KEYS), BF),
        0,
        2 * PACK * KEYS * 2,
    )(place, weights, gain)


def forward_kernel(place, rows_mine, rows_other, packed_mine, packed_other, out):
    rows = out.shape[0] * OWN
    total = None
    for block, packed in ((rows_mine, packed_mine), (rows_other, packed_other)):
        pieces = packed[LANE : LANE + 1, :].astype(F32)
        gains = pieces[:, :LANE] + pieces[:, LANE : 2 * LANE] + pieces[:, 2 * LANE : 3 * LANE]
        left = (block[...].reshape(rows, LANE).astype(F32) * gains).astype(BF)
        term = jnp.dot(left, packed[:LANE, :], preferred_element_type=F32)
        total = term if total is None else total + term
    out[...] = total.astype(BF).reshape(out.shape)


def forward(place, fresh, rows_other, packed_mine, packed_other):
    step = 4
    return call(
        forward_kernel,
        (N_T // 2 // step,),
        [
            pl.BlockSpec((step, 1, OWN, LANE), lambda i, place: (i, place[1], 0, 0)),
            pl.BlockSpec((step, OWN, LANE), lambda i, place: (i, 0, 0)),
            pl.BlockSpec((PACK, KEYS), lambda i, place: (0, 0)),
            pl.BlockSpec((PACK, KEYS), lambda i, place: (0, 0)),
        ],
        pl.BlockSpec((step, OWN, KEYS), lambda i, place: (i, 0, 0)),
        jax.ShapeDtypeStruct((N_T // 2, OWN, KEYS), BF),
        2 * TOK // 2 * 2 * LANE * KEYS,
        7 * 1024 * 1024,
    )(place, fresh, rows_other, packed_mine, packed_other)


def column(value):
    return value.reshape(value.shape[0] * OWN)[:, None]


def backward_kernel(place, cot, weights, older, gain, scale, *refs):
    *before, base, curve, weight_sum, gain_sum = refs
    first = (pl.program_id(0) == 0) & (pl.program_id(1) == 0)

    @pl.when(first)
    def _():
        if before:
            weight_sum[...] = before[2][...]
            gain_sum[...] = before[3][...]
        else:
            weight_sum[...] = jnp.zeros_like(weight_sum)
            gain_sum[...] = jnp.zeros_like(gain_sum)

    rows = Z_STEP * OWN
    keys = cot[...].reshape(rows, KEYS)
    wide = older[...].reshape(rows, LANE).astype(F32)
    row_scale = column(scale[...].reshape(Z_STEP, OWN))
    gains = gain[...]
    grad = row_scale * lax.dot_general(
        keys, weights[...], (((1,), (1,)), ((), ())), preferred_element_type=F32
    )
    scaled = wide * gains
    curve[...] = jnp.sum(
        (grad * scaled.astype(BF).astype(F32)).reshape(Z_STEP, OWN, LANE), axis=-1
    ).reshape(curve.shape)
    gain_sum[...] += jnp.sum(grad * wide, axis=0, keepdims=True)
    base[...] = (grad * gains).reshape(base.shape)
    weight_sum[...] += lax.dot_general(
        (scaled * row_scale).astype(BF), keys, (((0,), (0,)), ((), ())), preferred_element_type=F32
    )


def backward(place, cot, weights, older, gain, scale, which, before):
    def tokens(a, i, place):
        return (i, a, place[1] ^ which, 0, 0)

    def whole(a, i, place):
        return (0, 0)

    in_specs = [
        pl.BlockSpec((Z_STEP, 1, OWN, KEYS), lambda a, i, place: (i, a, 0, 0)),
        pl.BlockSpec((LANE, KEYS), whole),
        pl.BlockSpec((Z_STEP, 1, 1, OWN, LANE), tokens),
        pl.BlockSpec((1, LANE), whole),
        pl.BlockSpec((Z_STEP, 1, 1, 1, OWN), tokens),
    ]
    aliases = {}
    if before:
        in_specs += [
            pl.BlockSpec(memory_space=pl.ANY),
            pl.BlockSpec(memory_space=pl.ANY),
            pl.BlockSpec((LANE, KEYS), whole),
            pl.BlockSpec((1, LANE), whole),
        ]
        aliases = {6: 0, 7: 1}
    return call(
        backward_kernel,
        (2, N_Z // Z_STEP),
        in_specs,
        [
            pl.BlockSpec((Z_STEP, 1, 1, OWN, LANE), tokens),
            pl.BlockSpec((Z_STEP, 1, 1, 1, OWN), tokens),
            pl.BlockSpec((LANE, KEYS), whole),
            pl.BlockSpec((1, LANE), whole),
        ],
        [
            jax.ShapeDtypeStruct((N_Z, 2, 2, OWN, LANE), F32),
            jax.ShapeDtypeStruct((N_Z, 2, 2, 1, OWN), F32),
            jax.ShapeDtypeStruct((LANE, KEYS), F32),
            jax.ShapeDtypeStruct((1, LANE), F32),
        ],
        4 * (TOK // 2) * LANE * KEYS,
        9 * 1024 * 1024,
        aliases,
    )(place, cot, weights, older, gain, scale, *before)


def finish_kernel(place, early, late, base, older, pull, out):
    bent = base[...] - column(pull[0]) * older[...].astype(F32)
    down = jnp.where(pl.program_id(0) < N_Z // 2, early[...].astype(F32), late[...].astype(F32))
    out[...] = (down + bent).astype(BF)


def finish(place, early, late, base, older, pull):
    rows = TOK // N_Z
    mid = N_Z // 2
    block = pl.BlockSpec((rows, LANE), lambda i, place: (i, 0))
    return call(
        finish_kernel,
        (N_Z,),
        [
            pl.BlockSpec((rows, LANE), lambda i, place: (jnp.minimum(i, mid - 1), 0)),
            pl.BlockSpec((rows, LANE), lambda i, place: (jnp.maximum(i - mid, 0), 0)),
            block,
            block,
            pl.BlockSpec((1, rows // OWN, OWN), lambda i, place: (i, 0, 0)),
        ],
        block,
        jax.ShapeDtypeStruct((TOK, LANE), BF),
        0,
        10 * 1024 * 1024,
    )(place, early, late, base, older, pull)


def shards(upstream, stashed, returning, key_cotangent, key_weight, norm_gain, lengths):
    lane = lax.axis_index("ts")
    core = lane % 2
    half = (lane // 2) % 2
    z = lane // 4
    place = jnp.stack([half, core, z]).astype(jnp.int32)
    weights = key_weight[0]
    fresh = upstream[0]
    saved = stashed[0]

    packed = move(pack(place, weights, norm_gain), to_previous)

    lanes = [[q * 2 + c for q in range(N_T // 2)] for c in range(2)]
    cot_mine = lax.all_gather(key_cotangent[0], "ts", axis=0, axis_index_groups=lanes, tiled=True)

    fresh_wide = fresh.astype(F32)
    saved_wide = saved.astype(F32)
    fresh_part = jnp.sum(fresh_wide * fresh_wide, axis=1).reshape(N_Z, 2, 2, OWN)
    saved_part = jnp.sum(saved_wide * saved_wide, axis=1).reshape(1, N_T, OWN)
    squares = jnp.concatenate(
        [
            fresh_part.reshape(N_T, 1, OWN),
            fresh_part[:, ::-1].reshape(N_T, 1, OWN),
            jnp.broadcast_to(saved_part, (N_T, N_T, OWN)),
        ],
        axis=1,
    )
    squares = jnp.sum(lax.all_to_all(squares, "ts", 0, 0, tiled=True), axis=0)
    fresh_rate = lax.rsqrt(squares[:2] / WIDTH + eps)
    older_sq = move(squares[2:], to_mirror)

    older = move(after(saved, packed), to_mirror)
    early, late = lax.optimization_barrier((returning[0, : TOK // 2], returning[0, TOK // 2 :]))
    early = move(after(early, older, older_sq), to_previous)
    late = move(after(late, older, older_sq), to_previous)

    rows = fresh.reshape(N_T // 2, 2, OWN, LANE)
    rows_other = move(lax.dynamic_index_in_dim(rows, 1 - core, 1, keepdims=False), to_other_core)
    packed_other = move(packed, to_other_core)
    partial = forward(place, rows, rows_other, packed, after(packed_other, squares))

    def block(distance):
        return lax.dynamic_slice_in_dim(partial, ((z + distance) % N_Z) * 2, 2, 0)

    older_rate = lax.rsqrt(older_sq / WIDTH + eps)
    live = (jnp.arange(TOK, dtype=jnp.int32) < lengths[0]).astype(F32).reshape(N_T, OWN)
    scale = (live * older_rate).reshape(N_Z, 2, 2, 1, OWN)
    older_parts = older.reshape(N_Z, 2, 2, OWN, LANE)
    cot_mine = after(cot_mine, older, older_sq, partial)
    cot_other = move(cot_mine, to_other_core)
    cots = [value.reshape(N_Z, 2, OWN, KEYS) for value in (cot_mine, cot_other)]
    sums = backward(place, cots[0], weights, older_parts, norm_gain, scale, 0, [])
    base, curve, weight_total, gain_grad = backward(
        place, cots[1], weights, older_parts, norm_gain, scale, 1, sums
    )

    up = move(after(block(4), older), z_up, (0,))
    down = move(after(block(4), older), z_down, (1,))
    up, down = lax.optimization_barrier((up, down))
    up = move(add(block(3), up), z_up)
    down = move(add(block(-3), down), z_down)
    up, down = lax.optimization_barrier((up, down, sums[1], early))[:2]
    up = move(add(block(2), up), z_up)
    down = move(add(block(-2), down), z_down)
    up, down = lax.optimization_barrier((up, down, curve))[:2]
    up = move(add(block(1), up), z_up)
    down = move(add(block(-1), down), z_down)

    curve = jnp.broadcast_to(curve.astype(BF).reshape(1, N_T, OWN), (N_T, N_T, OWN))
    curve = jnp.sum(lax.all_to_all(curve, "ts", 0, 0, tiled=True).astype(F32), axis=0)
    pull = (older_rate * older_rate / WIDTH * curve).reshape(N_Z, N_T // N_Z, OWN)

    summed = block(0).astype(F32) + up.astype(F32) + after(down, pull, late).astype(F32)
    straight = move((pick(summed, half) * fresh_rate[0][:, None]).astype(BF), to_next)
    crossed = move((pick(summed, 1 - half) * fresh_rate[1][:, None]).astype(BF), to_next_other_half)
    new_keys = (straight.astype(F32) + crossed.astype(F32)).astype(BF)

    input_grad = finish(place, early, late, base.reshape(TOK, LANE), older, pull)
    return (new_keys[None], input_grad[None], weight_total[None], gain_grad)


def solution(mesh):
    return jax.shard_map(
        shards,
        mesh=mesh,
        in_specs=(
            P("section", None, "ts"),
            P("section", None, "ts"),
            P("section", None, "ts"),
            P("section", "ts", None),
            P("section", "ts", None),
            P("section", "ts"),
            P("section"),
        ),
        out_specs=(
            P("section", "ts", None),
            P("section", None, "ts"),
            P("section", "ts", None),
            P("section", "ts"),
        ),
        check_vma=False,
    )
```

```python
import jax
import jax.numpy as jnp
from jax import lax
from jax.experimental import pallas as pl
from jax.experimental.pallas import tpu as pltpu
from jax.sharding import PartitionSpec as P

eps = 1e-05
BF = jnp.bfloat16
F32 = jnp.float32
N_S = 8
N_T = 32
N_Z = 8
TOK = 4096
OWN = TOK // N_T
WIDTH = 8192
LANE = WIDTH // N_T
KEYS = 1024
PACK = LANE + 16
SPLIT = TOK // 2
AXES = ("section", "ts")


def move(value, target, cores=(0, 1)):
    pairs = []
    for s in range(N_S):
        for t in [t for t in range(N_T) if t % 2 in cores]:
            to_s, to_t = target(s, t)
            pairs.append((s * N_T + t, to_s * N_T + to_t))
    return lax.ppermute(value, AXES, pairs)


def to_next(s, t):
    return (s + 1) % N_S, t


def to_previous(s, t):
    return (s - 1) % N_S, t


def to_mirror(s, t):
    return N_S - 1 - s, t


def to_mirror_other_half(s, t):
    return N_S - 1 - s, t ^ 2


def to_other_core(s, t):
    return s, t ^ 1


def to_other_half(s, t):
    return s, t ^ 2


def to_next_other_half(s, t):
    return (s + 1) % N_S, t ^ 2


def z_up(s, t):
    return s, (t + 4) % N_T


def z_down(s, t):
    return s, (t - 4) % N_T


def pick(value, index):
    return lax.dynamic_index_in_dim(value, index, 0, keepdims=False)


def after(value, *others):
    return lax.optimization_barrier((value,) + others)[0]


def add(a, b):
    return (a.astype(F32) + b.astype(F32)).astype(BF)


def call(kernel, grid, in_specs, out_specs, out_shape, flops, size, scratch=()):
    return pl.pallas_call(
        kernel,
        grid_spec=pltpu.PrefetchScalarGridSpec(
            num_scalar_prefetch=1,
            grid=grid,
            in_specs=in_specs,
            out_specs=out_specs,
            scratch_shapes=scratch,
        ),
        out_shape=out_shape,
        compiler_params=pltpu.CompilerParams(vmem_limit_bytes=24 * 1024 * 1024),
        cost_estimate=pl.CostEstimate(flops=flops, bytes_accessed=size, transcendentals=0),
    )


def pack_kernel(place, weights, gain, out):
    out[:LANE, :] = weights[...]
    value = gain[...]
    high = value.astype(BF)
    middle = (value - high.astype(F32)).astype(BF)
    low = (value - high.astype(F32) - middle.astype(F32)).astype(BF)
    row = jnp.concatenate([high, middle, low, jnp.zeros((1, LANE), BF)], axis=1)
    out[LANE:, :] = jnp.broadcast_to(row, (PACK - LANE, KEYS))


def pack(place, weights, gain):
    return call(
        pack_kernel,
        (1,),
        [
            pl.BlockSpec((LANE, KEYS), lambda i, place: (0, 0)),
            pl.BlockSpec((1, LANE), lambda i, place: (0, 0)),
        ],
        pl.BlockSpec((PACK, KEYS), lambda i, place: (0, 0)),
        jax.ShapeDtypeStruct((PACK, KEYS), BF),
        0,
        2 * PACK * KEYS * 2,
    )(place, weights, gain)


def forward_kernel(place, rows_mine, rows_other, packed_mine, packed_other, out, weights):
    rows = out.shape[0] * OWN

    @pl.when(pl.program_id(0) == 0)
    def _():
        weights[:LANE, :] = packed_mine[:LANE, :]
        weights[LANE:, :] = packed_other[:LANE, :]

    left = []
    for block, packed in ((rows_mine, packed_mine), (rows_other, packed_other)):
        pieces = packed[LANE : LANE + 1, :].astype(F32)
        gains = pieces[:, :LANE] + pieces[:, LANE : 2 * LANE] + pieces[:, 2 * LANE : 3 * LANE]
        left.append((block[...].reshape(rows, LANE).astype(F32) * gains).astype(BF))
    total = jnp.dot(jnp.concatenate(left, axis=1), weights[...], preferred_element_type=F32)
    out[...] = total.astype(BF).reshape(out.shape)


def forward(place, fresh, rows_other, packed_mine, packed_other):
    step = 4
    return call(
        forward_kernel,
        (N_T // 2 // step,),
        [
            pl.BlockSpec((step, 1, OWN, LANE), lambda i, place: (i, place[0], 0, 0)),
            pl.BlockSpec((step, OWN, LANE), lambda i, place: (i, 0, 0)),
            pl.BlockSpec((PACK, KEYS), lambda i, place: (0, 0)),
            pl.BlockSpec((PACK, KEYS), lambda i, place: (0, 0)),
        ],
        pl.BlockSpec((step, OWN, KEYS), lambda i, place: (i, 0, 0)),
        jax.ShapeDtypeStruct((N_T // 2, OWN, KEYS), BF),
        2 * TOK // 2 * 2 * LANE * KEYS,
        7 * 1024 * 1024,
        [pltpu.VMEM((2 * LANE, KEYS), BF)],
    )(place, fresh, rows_other, packed_mine, packed_other)


def shards(upstream, stashed, returning, key_cotangent, key_weight, norm_gain, lengths):
    lane = lax.axis_index("ts")
    core = lane % 2
    half = (lane // 2) % 2
    z = lane // 4
    place = core.astype(jnp.int32)[None]
    gain = norm_gain[0]
    weights = key_weight[0]
    fresh = upstream[0]
    saved = stashed[0]

    def by_core(value):
        parts = value.reshape(N_T // 2, 2, OWN, *value.shape[1:])
        return [
            lax.dynamic_index_in_dim(parts, index, 1, keepdims=False).reshape(
                TOK // 2, *value.shape[1:]
            )
            for index in (core, 1 - core)
        ]

    fresh_wide = fresh.astype(F32)
    saved_wide = saved.astype(F32)
    fresh_part = jnp.sum(fresh_wide * fresh_wide, axis=1).reshape(N_Z, 2, 2, OWN)
    saved_part = jnp.sum(saved_wide * saved_wide, axis=1).reshape(1, N_T, OWN)
    squares = jnp.concatenate(
        [
            fresh_part.reshape(N_T, 1, OWN).astype(BF),
            fresh_part[:, ::-1].reshape(N_T, 1, OWN).astype(BF),
            jnp.broadcast_to(saved_part.astype(BF), (N_T, N_T, OWN)),
        ],
        axis=1,
    )
    squares = lax.all_to_all(squares, "ts", 0, 0, tiled=True)

    packed = move(after(pack(place, weights, norm_gain), squares), to_previous)
    squares = jnp.sum(squares.astype(F32), axis=0)
    fresh_rate = lax.rsqrt(squares[:2] / WIDTH + eps)
    older_sq = move(squares[2:], to_mirror)

    cot_own = key_cotangent[0]
    cot_half = move(cot_own, to_other_half)
    cot_pair = jnp.stack(
        [jnp.where(half == 0, cot_own, cot_half), jnp.where(half == 0, cot_half, cot_own)]
    )
    lanes = [[q * 4 + j for q in range(N_Z)] for j in range(4)]
    cot_mine = lax.all_gather(cot_pair, "ts", axis=0, axis_index_groups=lanes, tiled=True)
    cot_mine = cot_mine.reshape(TOK // 2, KEYS)

    older = move(after(saved, squares), to_mirror)

    rows = fresh.reshape(N_T // 2, 2, OWN, LANE)
    rows_other = move(lax.dynamic_index_in_dim(rows, 1 - core, 1, keepdims=False), to_other_core)
    packed_other = move(packed, to_other_core)
    partial = forward(place, rows, rows_other, packed, packed_other)

    def block(distance):
        return lax.dynamic_slice_in_dim(partial, ((z + distance) % N_Z) * 2, 2, 0)

    up = move(block(4), z_up, (0,))
    down = move(block(4), z_down, (1,))
    up, down = lax.optimization_barrier((up, down))
    up = move(add(block(3), up), z_up)
    down = move(add(block(-3), down), z_down)
    up, down = lax.optimization_barrier((up, down, older))[:2]
    up = add(block(2), up)
    down = add(block(-2), down)

    cot_mine, older_sq = lax.optimization_barrier((cot_mine, older_sq, up, down, older))[:2]
    early = move(after(returning[0, :SPLIT], older, older_sq), to_previous)
    late = move(after(returning[0, SPLIT:], older, older_sq), to_previous)
    up = move(up, z_up)
    down = move(down, z_down)
    cots = [cot_mine, after(move(cot_mine, to_other_core), early)]
    older_rate = lax.rsqrt(older_sq / WIDTH + eps).reshape(TOK)
    live = (jnp.arange(TOK, dtype=jnp.int32) < lengths[0]).astype(F32)
    scales = by_core(live * older_rate)
    raw = [
        lax.dot_general(cot, weights, (((1,), (1,)), ((), ())), preferred_element_type=F32)
        for cot in cots
    ]
    up, down, raw[0] = lax.optimization_barrier((up, down, raw[0]))
    up = move(add(block(1), up), z_up)
    down = move(add(block(-1), down), z_down)
    grads = []
    curves = []
    weight_total = jnp.zeros((LANE, KEYS), F32)
    gain_grad = jnp.zeros((LANE,), F32)
    for cot, product, rows, scale in zip(cots, raw, by_core(older), scales):
        wide = rows.astype(F32)
        grad = scale[:, None] * product
        grads.append(grad)
        curves.append(jnp.sum(grad * (wide * gain).astype(BF).astype(F32), axis=1))
        gain_grad = gain_grad + jnp.sum(grad * wide, axis=0)
        weight_total = weight_total + lax.dot_general(
            (wide * gain * scale[:, None]).astype(BF),
            cot,
            (((0,), (0,)), ((), ())),
            preferred_element_type=F32,
        )

    mine = (jnp.arange(2) == core)[None, :, None]
    curve = [part.reshape(N_T // 2, 1, OWN) for part in curves]
    curve = jnp.where(mine, curve[0], curve[1])
    curve = jnp.broadcast_to(curve.reshape(1, N_T, OWN).astype(BF), (N_T, N_T, OWN))
    curve = lax.all_to_all(curve, "ts", 0, 0, tiled=True)
    up, down = lax.optimization_barrier((up, down, curve, late))[:2]
    curve = jnp.sum(curve.astype(F32), axis=0).reshape(TOK)
    pull = older_rate * older_rate / WIDTH * curve

    summed = block(0).astype(F32) + up.astype(F32) + down.astype(F32)
    straight = move((pick(summed, half) * fresh_rate[0][:, None]).astype(BF), to_next)
    crossed = move(
        (pick(summed, 1 - half) * fresh_rate[1][:, None]).astype(BF), to_next_other_half
    )
    new_keys = (straight.astype(F32) + crossed.astype(F32)).astype(BF)

    base = [(gain * grad).reshape(N_T // 2, 1, OWN, LANE) for grad in grads]
    base = jnp.where(mine[..., None], base[0], base[1]).reshape(TOK, LANE)
    downstream = jnp.concatenate([early, late], axis=0)
    total = downstream.astype(F32) + base - pull[:, None] * older.astype(F32)
    return (
        new_keys[None],
        total.astype(BF)[None],
        weight_total[None],
        gain_grad[None],
    )


def solution(mesh):
    return jax.shard_map(
        shards,
        mesh=mesh,
        in_specs=(
            P("section", None, "ts"),
            P("section", None, "ts"),
            P("section", None, "ts"),
            P("section", "ts", None),
            P("section", "ts", None),
            P("section", "ts"),
            P("section"),
        ),
        out_specs=(
            P("section", "ts", None),
            P("section", None, "ts"),
            P("section", "ts", None),
            P("section", "ts"),
        ),
        check_vma=False,
    )
```

```python
import jax
import jax.numpy as jnp
from jax import lax
from jax.experimental import pallas as pl
from jax.experimental.pallas import tpu as pltpu
from jax.sharding import PartitionSpec as P

eps = 1e-05
BF = jnp.bfloat16
F32 = jnp.float32
N_S = 8
N_T = 32
N_Z = 8
TOK = 4096
OWN = TOK // N_T
WIDTH = 8192
LANE = WIDTH // N_T
KEYS = 1024
PACK = LANE + 16
SPLIT = (TOK // 4, 5 * TOK // 8)
AXES = ("section", "ts")


def move(value, target, cores=(0, 1)):
    pairs = []
    for s in range(N_S):
        for t in [t for t in range(N_T) if t % 2 in cores]:
            to_s, to_t = target(s, t)
            pairs.append((s * N_T + t, to_s * N_T + to_t))
    return lax.ppermute(value, AXES, pairs)


def to_next(s, t):
    return (s + 1) % N_S, t


def to_previous(s, t):
    return (s - 1) % N_S, t


def to_mirror(s, t):
    return N_S - 1 - s, t


def to_mirror_other_half(s, t):
    return N_S - 1 - s, t ^ 2


def to_other_core(s, t):
    return s, t ^ 1


def to_other_half(s, t):
    return s, t ^ 2


def to_next_other_half(s, t):
    return (s + 1) % N_S, t ^ 2


def z_up(s, t):
    return s, (t + 4) % N_T


def z_down(s, t):
    return s, (t - 4) % N_T


def pick(value, index):
    return lax.dynamic_index_in_dim(value, index, 0, keepdims=False)


def after(value, *others):
    return lax.optimization_barrier((value,) + others)[0]


def add(a, b):
    return (a.astype(F32) + b.astype(F32)).astype(BF)


def call(kernel, grid, in_specs, out_specs, out_shape, flops, size, scratch=()):
    return pl.pallas_call(
        kernel,
        grid_spec=pltpu.PrefetchScalarGridSpec(
            num_scalar_prefetch=1,
            grid=grid,
            in_specs=in_specs,
            out_specs=out_specs,
            scratch_shapes=scratch,
        ),
        out_shape=out_shape,
        compiler_params=pltpu.CompilerParams(vmem_limit_bytes=24 * 1024 * 1024),
        cost_estimate=pl.CostEstimate(flops=flops, bytes_accessed=size, transcendentals=0),
    )


def pack_kernel(place, weights, gain, out):
    out[:LANE, :] = weights[...]
    value = gain[...]
    high = value.astype(BF)
    middle = (value - high.astype(F32)).astype(BF)
    low = (value - high.astype(F32) - middle.astype(F32)).astype(BF)
    row = jnp.concatenate([high, middle, low, jnp.zeros((1, LANE), BF)], axis=1)
    out[LANE:, :] = jnp.broadcast_to(row, (PACK - LANE, KEYS))


def pack(place, weights, gain):
    return call(
        pack_kernel,
        (1,),
        [
            pl.BlockSpec((LANE, KEYS), lambda i, place: (0, 0)),
            pl.BlockSpec((1, LANE), lambda i, place: (0, 0)),
        ],
        pl.BlockSpec((PACK, KEYS), lambda i, place: (0, 0)),
        jax.ShapeDtypeStruct((PACK, KEYS), BF),
        0,
        2 * PACK * KEYS * 2,
    )(place, weights, gain)


def forward_kernel(place, rows_mine, rows_other, packed_mine, packed_other, out, weights):
    rows = out.shape[0] * OWN

    @pl.when(pl.program_id(0) == 0)
    def _():
        weights[:LANE, :] = packed_mine[:LANE, :]
        weights[LANE:, :] = packed_other[:LANE, :]

    left = []
    for block, packed in ((rows_mine, packed_mine), (rows_other, packed_other)):
        pieces = packed[LANE : LANE + 1, :].astype(F32)
        gains = pieces[:, :LANE] + pieces[:, LANE : 2 * LANE] + pieces[:, 2 * LANE : 3 * LANE]
        left.append((block[...].reshape(rows, LANE).astype(F32) * gains).astype(BF))
    total = jnp.dot(jnp.concatenate(left, axis=1), weights[...], preferred_element_type=F32)
    out[...] = total.astype(BF).reshape(out.shape)


def forward(place, fresh, rows_other, packed_mine, packed_other):
    step = 4
    return call(
        forward_kernel,
        (N_T // 2 // step,),
        [
            pl.BlockSpec((step, 1, OWN, LANE), lambda i, place: (i, place[0], 0, 0)),
            pl.BlockSpec((step, OWN, LANE), lambda i, place: (i, 0, 0)),
            pl.BlockSpec((PACK, KEYS), lambda i, place: (0, 0)),
            pl.BlockSpec((PACK, KEYS), lambda i, place: (0, 0)),
        ],
        pl.BlockSpec((step, OWN, KEYS), lambda i, place: (i, 0, 0)),
        jax.ShapeDtypeStruct((N_T // 2, OWN, KEYS), BF),
        2 * TOK // 2 * 2 * LANE * KEYS,
        7 * 1024 * 1024,
        [pltpu.VMEM((2 * LANE, KEYS), BF)],
    )(place, fresh, rows_other, packed_mine, packed_other)


def shards(upstream, stashed, returning, key_cotangent, key_weight, norm_gain, lengths):
    lane = lax.axis_index("ts")
    core = lane % 2
    half = (lane // 2) % 2
    z = lane // 4
    place = core.astype(jnp.int32)[None]
    gain = norm_gain[0]
    weights = key_weight[0]
    fresh = upstream[0]
    saved = stashed[0]

    def by_core(value):
        parts = value.reshape(N_T // 2, 2, OWN, *value.shape[1:])
        return [
            lax.dynamic_index_in_dim(parts, index, 1, keepdims=False).reshape(
                TOK // 2, *value.shape[1:]
            )
            for index in (core, 1 - core)
        ]

    packed = pack(place, weights, norm_gain)
    packed, fresh_rows = lax.optimization_barrier((packed, fresh))
    packed = move(packed, to_previous)

    cot_own = key_cotangent[0]
    cot_half = move(cot_own, to_other_half)
    cot_pair = jnp.stack(
        [jnp.where(half == 0, cot_own, cot_half), jnp.where(half == 0, cot_half, cot_own)]
    )
    lanes = [[q * 4 + j for q in range(N_Z)] for j in range(4)]
    cot_mine = lax.all_gather(cot_pair, "ts", axis=0, axis_index_groups=lanes, tiled=True)
    cot_mine = cot_mine.reshape(TOK // 2, KEYS)

    older_first = move(after(saved[: TOK // 2], cot_half), to_mirror)

    rows = fresh.reshape(N_T // 2, 2, OWN, LANE)
    rows_other = fresh_rows.reshape(N_T // 2, 2, OWN, LANE)
    rows_other = move(
        lax.dynamic_index_in_dim(rows_other, 1 - core, 1, keepdims=False), to_other_core
    )

    fresh_wide = fresh.astype(F32)
    saved_wide = saved.astype(F32)
    fresh_part = jnp.sum(fresh_wide * fresh_wide, axis=1).reshape(N_Z, 2, 2, OWN)
    saved_part = jnp.sum(saved_wide * saved_wide, axis=1).reshape(1, N_T, OWN)
    squares = jnp.concatenate(
        [
            fresh_part.transpose(0, 2, 1, 3).reshape(N_T // 2, 2, OWN).astype(BF),
            jnp.broadcast_to(saved_part.astype(BF), (N_T // 2, N_T, OWN)),
        ],
        axis=1,
    )
    halves = [[q * 4 + h * 2 + c for q in range(N_Z) for c in range(2)] for h in range(2)]
    squares = lax.all_to_all(
        after(squares, rows_other), "ts", 0, 0, axis_index_groups=halves, tiled=True
    )
    squares_raw = squares
    squares = jnp.sum(squares.astype(F32), axis=0)
    older_sq = [move(squares[2:], to_mirror), move(squares[2:], to_mirror_other_half)]
    fresh_other = move(after(squares[:2], *older_sq), to_other_half)

    older_second = move(after(saved[TOK // 2 :], *older_sq), to_mirror)

    parts = [
        move(after(returning[0, begin:end], *older_sq), to_previous)
        for begin, end in zip((0,) + SPLIT, SPLIT + (TOK,))
    ]

    packed_other = move(packed, to_other_core)
    partial = forward(place, rows, rows_other, packed, packed_other)

    def block(distance):
        return lax.dynamic_slice_in_dim(partial, ((z + distance) % N_Z) * 2, 2, 0)

    far = after(block(4), squares_raw)
    up = move(far, z_up, (0,))
    down = move(far, z_down, (1,))
    up, down = lax.optimization_barrier((up, down, older_first))[:2]
    up = move(add(block(3), up), z_up)
    down = move(add(block(-3), down), z_down)
    up, down = lax.optimization_barrier((up, down, older_second, parts[0]))[:2]
    up = add(block(2), up)
    down = add(block(-2), down)

    older = jnp.concatenate([older_first, older_second], axis=0)
    cot_mine, *older_sq = lax.optimization_barrier((cot_mine, *older_sq, up, down))[:3]
    up = move(up, z_up)
    down = move(down, z_down)
    cots = [cot_mine, move(cot_mine, to_other_core)]
    older_rate = lax.rsqrt((older_sq[0] + older_sq[1]) / WIDTH + eps).reshape(TOK)
    live = (jnp.arange(TOK, dtype=jnp.int32) < lengths[0]).astype(F32)
    scales = by_core(live * older_rate)
    raw = [
        lax.dot_general(cot, weights, (((1,), (1,)), ((), ())), preferred_element_type=F32)
        for cot in cots
    ]
    up, down, raw[0] = lax.optimization_barrier((up, down, raw[0]))
    up, down = lax.optimization_barrier((up, down, parts[1]))[:2]
    up = move(add(block(1), up), z_up)
    down = move(add(block(-1), down), z_down)
    grads = []
    curves = []
    weight_total = jnp.zeros((LANE, KEYS), F32)
    gain_grad = jnp.zeros((LANE,), F32)
    for cot, product, rows, scale in zip(cots, raw, by_core(older), scales):
        wide = rows.astype(F32)
        grad = scale[:, None] * product
        grads.append(grad)
        curves.append(jnp.sum(grad * (wide * gain).astype(BF).astype(F32), axis=1))
        gain_grad = gain_grad + jnp.sum(grad * wide, axis=0)
        weight_total = weight_total + lax.dot_general(
            (wide * gain * scale[:, None]).astype(BF),
            cot,
            (((0,), (0,)), ((), ())),
            preferred_element_type=F32,
        )

    mine = (jnp.arange(2) == core)[None, :, None]
    curve = [part.reshape(N_T // 2, 1, OWN) for part in curves]
    curve = jnp.where(mine, curve[0], curve[1])
    curve = jnp.broadcast_to(curve.reshape(1, N_T, OWN).astype(BF), (N_T, N_T, OWN))
    curve = lax.all_to_all(curve, "ts", 0, 0, tiled=True)
    up, down, fresh_other = lax.optimization_barrier((up, down, fresh_other, curve, parts[2]))[:3]
    fresh_rate = lax.rsqrt((squares[:2] + fresh_other) / WIDTH + eps)
    curve = jnp.sum(curve.astype(F32), axis=0).reshape(TOK)
    pull = older_rate * older_rate / WIDTH * curve

    summed = block(0).astype(F32) + up.astype(F32) + down.astype(F32)
    straight = move((pick(summed, half) * pick(fresh_rate, half)[:, None]).astype(BF), to_next)
    crossed = move(
        (pick(summed, 1 - half) * pick(fresh_rate, 1 - half)[:, None]).astype(BF), to_next_other_half
    )
    new_keys = (straight.astype(F32) + crossed.astype(F32)).astype(BF)

    base = jnp.zeros((N_T // 2, 2, OWN, LANE), F32)
    for index, grad in zip((core, 1 - core), grads):
        base = lax.dynamic_update_index_in_dim(
            base, (gain * grad).reshape(N_T // 2, OWN, LANE), index, 1
        )
    base = base.reshape(TOK, LANE)
    downstream = jnp.concatenate(parts, axis=0)
    total = downstream.astype(F32) + base - pull[:, None] * older.astype(F32)
    return (
        new_keys[None],
        total.astype(BF)[None],
        weight_total[None],
        gain_grad[None],
    )


def solution(mesh):
    return jax.shard_map(
        shards,
        mesh=mesh,
        in_specs=(
            P("section", None, "ts"),
            P("section", None, "ts"),
            P("section", None, "ts"),
            P("section", "ts", None),
            P("section", "ts", None),
            P("section", "ts"),
            P("section"),
        ),
        out_specs=(
            P("section", "ts", None),
            P("section", None, "ts"),
            P("section", "ts", None),
            P("section", "ts"),
        ),
        check_vma=False,
    )
```

```python
import jax
import jax.numpy as jnp
from jax import lax
from jax.experimental import pallas as pl
from jax.experimental.pallas import tpu as pltpu
from jax.sharding import PartitionSpec as P

eps = 1e-05
BF = jnp.bfloat16
F32 = jnp.float32
N_S = 8
N_T = 32
N_Z = 8
TOK = 4096
OWN = TOK // N_T
WIDTH = 8192
LANE = WIDTH // N_T
KEYS = 1024
PACK = LANE + 16
CUT = 3 * TOK // 4
SPLIT = TOK // 4
AXES = ("section", "ts")


def move(value, target, cores=(0, 1)):
    pairs = []
    for s in range(N_S):
        for t in [t for t in range(N_T) if t % 2 in cores]:
            to_s, to_t = target(s, t)
            pairs.append((s * N_T + t, to_s * N_T + to_t))
    return lax.ppermute(value, AXES, pairs)


def to_next(s, t):
    return (s + 1) % N_S, t


def to_previous(s, t):
    return (s - 1) % N_S, t


def to_mirror(s, t):
    return N_S - 1 - s, t


def to_mirror_other_half(s, t):
    return N_S - 1 - s, t ^ 2


def to_other_core(s, t):
    return s, t ^ 1


def to_other_half(s, t):
    return s, t ^ 2


def to_next_other_half(s, t):
    return (s + 1) % N_S, t ^ 2


def z_up(s, t):
    return s, (t + 4) % N_T


def z_down(s, t):
    return s, (t - 4) % N_T


def pick(value, index):
    return lax.dynamic_index_in_dim(value, index, 0, keepdims=False)


def after(value, *others):
    return lax.optimization_barrier((value,) + others)[0]


def add(a, b):
    return (a.astype(F32) + b.astype(F32)).astype(BF)


def call(kernel, grid, in_specs, out_specs, out_shape, flops, size, scratch=()):
    return pl.pallas_call(
        kernel,
        grid_spec=pltpu.PrefetchScalarGridSpec(
            num_scalar_prefetch=1,
            grid=grid,
            in_specs=in_specs,
            out_specs=out_specs,
            scratch_shapes=scratch,
        ),
        out_shape=out_shape,
        compiler_params=pltpu.CompilerParams(vmem_limit_bytes=24 * 1024 * 1024),
        cost_estimate=pl.CostEstimate(flops=flops, bytes_accessed=size, transcendentals=0),
    )


def pack_kernel(place, weights, gain, out):
    out[:LANE, :] = weights[...]
    value = gain[...]
    high = value.astype(BF)
    middle = (value - high.astype(F32)).astype(BF)
    low = (value - high.astype(F32) - middle.astype(F32)).astype(BF)
    row = jnp.concatenate([high, middle, low, jnp.zeros((1, LANE), BF)], axis=1)
    out[LANE:, :] = jnp.broadcast_to(row, (PACK - LANE, KEYS))


def pack(place, weights, gain):
    return call(
        pack_kernel,
        (1,),
        [
            pl.BlockSpec((LANE, KEYS), lambda i, place: (0, 0)),
            pl.BlockSpec((1, LANE), lambda i, place: (0, 0)),
        ],
        pl.BlockSpec((PACK, KEYS), lambda i, place: (0, 0)),
        jax.ShapeDtypeStruct((PACK, KEYS), BF),
        0,
        2 * PACK * KEYS * 2,
    )(place, weights, gain)


def forward_kernel(place, rows_mine, rows_other, packed_mine, packed_other, out, weights):
    rows = out.shape[0] * OWN

    @pl.when(pl.program_id(0) == 0)
    def _():
        weights[:LANE, :] = packed_mine[:LANE, :]
        weights[LANE:, :] = packed_other[:LANE, :]

    left = []
    for block, packed in ((rows_mine, packed_mine), (rows_other, packed_other)):
        pieces = packed[LANE : LANE + 1, :].astype(F32)
        gains = pieces[:, :LANE] + pieces[:, LANE : 2 * LANE] + pieces[:, 2 * LANE : 3 * LANE]
        left.append((block[...].reshape(rows, LANE).astype(F32) * gains).astype(BF))
    total = jnp.dot(jnp.concatenate(left, axis=1), weights[...], preferred_element_type=F32)
    out[...] = total.astype(BF).reshape(out.shape)


def forward(place, fresh, rows_other, packed_mine, packed_other):
    step = 4
    return call(
        forward_kernel,
        (N_T // 2 // step,),
        [
            pl.BlockSpec((step, 1, OWN, LANE), lambda i, place: (i, place[0], 0, 0)),
            pl.BlockSpec((step, OWN, LANE), lambda i, place: (i, 0, 0)),
            pl.BlockSpec((PACK, KEYS), lambda i, place: (0, 0)),
            pl.BlockSpec((PACK, KEYS), lambda i, place: (0, 0)),
        ],
        pl.BlockSpec((step, OWN, KEYS), lambda i, place: (i, 0, 0)),
        jax.ShapeDtypeStruct((N_T // 2, OWN, KEYS), BF),
        2 * TOK // 2 * 2 * LANE * KEYS,
        7 * 1024 * 1024,
        [pltpu.VMEM((2 * LANE, KEYS), BF)],
    )(place, fresh, rows_other, packed_mine, packed_other)


def shards(upstream, stashed, returning, key_cotangent, key_weight, norm_gain, lengths):
    lane = lax.axis_index("ts")
    core = lane % 2
    half = (lane // 2) % 2
    z = lane // 4
    place = core.astype(jnp.int32)[None]
    gain = norm_gain[0]
    weights = key_weight[0]
    fresh = upstream[0]
    saved = stashed[0]

    def by_core(value):
        parts = value.reshape(N_T // 2, 2, OWN, *value.shape[1:])
        return [
            lax.dynamic_index_in_dim(parts, index, 1, keepdims=False).reshape(
                TOK // 2, *value.shape[1:]
            )
            for index in (core, 1 - core)
        ]

    packed = pack(place, weights, norm_gain)
    packed, fresh_rows = lax.optimization_barrier((packed, fresh))
    packed = move(packed, to_previous)

    cot_own = key_cotangent[0]
    cot_half = move(cot_own, to_other_half)
    cot_pair = jnp.stack(
        [jnp.where(half == 0, cot_own, cot_half), jnp.where(half == 0, cot_half, cot_own)]
    )
    lanes = [[q * 4 + j for q in range(N_Z)] for j in range(4)]
    cot_mine = lax.all_gather(cot_pair, "ts", axis=0, axis_index_groups=lanes, tiled=True)
    cot_mine = cot_mine.reshape(TOK // 2, KEYS)

    older_first = move(after(saved[:CUT], cot_half), to_mirror)

    rows = fresh.reshape(N_T // 2, 2, OWN, LANE)
    rows_other = fresh_rows.reshape(N_T // 2, 2, OWN, LANE)
    rows_other = move(
        lax.dynamic_index_in_dim(rows_other, 1 - core, 1, keepdims=False), to_other_core
    )

    fresh_wide = fresh.astype(F32)
    saved_wide = saved.astype(F32)
    fresh_part = jnp.sum(fresh_wide * fresh_wide, axis=1).reshape(N_Z, 2, 2, OWN)
    saved_part = jnp.sum(saved_wide * saved_wide, axis=1).reshape(1, N_T, OWN)
    squares = jnp.concatenate(
        [
            fresh_part.transpose(0, 2, 1, 3).reshape(N_T // 2, 2, OWN).astype(BF),
            jnp.broadcast_to(saved_part.astype(BF), (N_T // 2, N_T, OWN)),
        ],
        axis=1,
    )
    halves = [[q * 4 + h * 2 + c for q in range(N_Z) for c in range(2)] for h in range(2)]
    squares = lax.all_to_all(
        after(squares, packed), "ts", 0, 0, axis_index_groups=halves, tiled=True
    )
    squares_raw = squares
    squares = jnp.sum(squares.astype(F32), axis=0)
    older_sq = [move(squares[2:], to_mirror), move(squares[2:], to_mirror_other_half)]
    fresh_other = move(after(squares[:2], *older_sq), to_other_half)

    older_second = move(after(saved[CUT:], *older_sq), to_mirror)

    early = move(after(returning[0, :SPLIT], *older_sq), to_previous)
    late = returning[0, SPLIT:]

    packed_other = move(packed, to_other_core)
    partial = forward(place, rows, rows_other, packed, packed_other)

    def block(distance):
        return lax.dynamic_slice_in_dim(partial, ((z + distance) % N_Z) * 2, 2, 0)

    up = move(block(4), z_up, (0,))
    down = move(block(4), z_down, (1,))
    base = jnp.zeros((N_T // 2, 2, OWN, LANE), F32)
    up, down, base, late = lax.optimization_barrier(
        (up, down, base, late, squares_raw, older_first, *older_sq)
    )[:4]
    late = move(after(late, early), to_previous)
    up = add(block(3), up)
    down = add(block(-3), down)
    up = move(up, z_up)
    down = move(down, z_down)
    up, down, cot_mine = lax.optimization_barrier((up, down, cot_mine, older_second, early))[:3]

    cots = [cot_mine, move(cot_mine, to_other_core)]
    raw = [
        lax.dot_general(cot, weights, (((1,), (1,)), ((), ())), preferred_element_type=F32)
        for cot in cots
    ]
    up = add(block(2), up)
    down = add(block(-2), down)
    older_first, older_second, *older_sq = lax.optimization_barrier(
        (older_first, older_second, *older_sq, up, down)
    )[:4]
    up = move(up, z_up)
    down = move(down, z_down)
    up, down, *raw = lax.optimization_barrier((up, down, *raw))
    up = add(block(1), up)
    down = add(block(-1), down)
    up, down, *raw = lax.optimization_barrier((up, down, *raw))
    up = move(up, z_up)
    down = move(down, z_down)
    older = jnp.concatenate([older_first, older_second], axis=0)
    older_rate = lax.rsqrt((older_sq[0] + older_sq[1]) / WIDTH + eps).reshape(TOK)
    live = (jnp.arange(TOK, dtype=jnp.int32) < lengths[0]).astype(F32)
    scales = by_core(live * older_rate)
    grads = []
    curves = []
    lefts = []
    gain_grad = jnp.zeros((LANE,), F32)
    for cot, product, rows, scale in zip(cots, raw, by_core(older), scales):
        wide = rows.astype(F32)
        grad = scale[:, None] * product
        grads.append(grad)
        curves.append(jnp.sum(grad * (wide * gain).astype(BF).astype(F32), axis=1))
        gain_grad = gain_grad + jnp.sum(grad * wide, axis=0)
        lefts.append(wide * gain * scale[:, None])

    mine = (jnp.arange(2) == core)[None, :, None]
    curve = [part.reshape(N_T // 2, 1, OWN) for part in curves]
    curve = jnp.where(mine, curve[0], curve[1])
    curve = jnp.broadcast_to(curve.reshape(1, N_T, OWN).astype(BF), (N_T, N_T, OWN))
    curve = lax.all_to_all(curve, "ts", 0, 0, tiled=True)
    up, down, fresh_other = lax.optimization_barrier((up, down, fresh_other, curve))[:3]
    fresh_rate = lax.rsqrt((squares[:2] + fresh_other) / WIDTH + eps)
    curve = jnp.sum(curve.astype(F32), axis=0).reshape(TOK)
    pull = older_rate * older_rate / WIDTH * curve

    summed = block(0).astype(F32) + up.astype(F32) + down.astype(F32)
    straight = (pick(summed, half) * pick(fresh_rate, half)[:, None]).astype(BF)
    crossed = (pick(summed, 1 - half) * pick(fresh_rate, 1 - half)[:, None]).astype(BF)
    *cots, pull = lax.optimization_barrier((*cots, pull, straight, crossed))[:3]
    straight = move(straight, to_next)
    crossed = move(crossed, to_next_other_half)
    new_keys = (straight.astype(F32) + crossed.astype(F32)).astype(BF)

    weight_total = sum(
        lax.dot_general(
            left.astype(BF), cot, (((0,), (0,)), ((), ())), preferred_element_type=F32
        )
        for left, cot in zip(lefts, cots)
    )
    for index, grad in zip((core, 1 - core), grads):
        base = lax.dynamic_update_index_in_dim(
            base, (gain * grad).reshape(N_T // 2, OWN, LANE), index, 1
        )
    base = base.reshape(TOK, LANE)
    downstream = jnp.concatenate([early, late], axis=0)
    total = downstream.astype(F32) + base - pull[:, None] * older.astype(F32)
    return (
        new_keys[None],
        total.astype(BF)[None],
        weight_total[None],
        gain_grad[None],
    )


def solution(mesh):
    return jax.shard_map(
        shards,
        mesh=mesh,
        in_specs=(
            P("section", None, "ts"),
            P("section", None, "ts"),
            P("section", None, "ts"),
            P("section", "ts", None),
            P("section", "ts", None),
            P("section", "ts"),
            P("section"),
        ),
        out_specs=(
            P("section", "ts", None),
            P("section", None, "ts"),
            P("section", "ts", None),
            P("section", "ts"),
        ),
        check_vma=False,
    )
```

```python
import jax
import jax.numpy as jnp
from jax import lax
from jax.experimental import pallas as pl
from jax.experimental.pallas import tpu as pltpu
from jax.sharding import PartitionSpec as P

eps = 1e-05
BF = jnp.bfloat16
F32 = jnp.float32
N_S = 8
N_T = 32
N_Z = 8
TOK = 4096
OWN = TOK // N_T
WIDTH = 8192
LANE = WIDTH // N_T
KEYS = 1024
PACK = LANE + 16
CUT = 3 * TOK // 4
SPLIT = TOK // 4
AXES = ("section", "ts")


def move(value, target, cores=(0, 1)):
    pairs = []
    for s in range(N_S):
        for t in [t for t in range(N_T) if t % 2 in cores]:
            to_s, to_t = target(s, t)
            pairs.append((s * N_T + t, to_s * N_T + to_t))
    return lax.ppermute(value, AXES, pairs)


def to_next(s, t):
    return (s + 1) % N_S, t


def to_previous(s, t):
    return (s - 1) % N_S, t


def to_mirror(s, t):
    return N_S - 1 - s, t


def to_mirror_other_half(s, t):
    return N_S - 1 - s, t ^ 2


def to_other_core(s, t):
    return s, t ^ 1


def to_other_half(s, t):
    return s, t ^ 2


def to_next_other_half(s, t):
    return (s + 1) % N_S, t ^ 2


def z_up(s, t):
    return s, (t + 4) % N_T


def z_down(s, t):
    return s, (t - 4) % N_T


def pick(value, index):
    return lax.dynamic_index_in_dim(value, index, 0, keepdims=False)


def after(value, *others):
    return lax.optimization_barrier((value,) + others)[0]


def add(a, b):
    return (a.astype(F32) + b.astype(F32)).astype(BF)


def call(kernel, grid, in_specs, out_specs, out_shape, flops, size, scratch=()):
    return pl.pallas_call(
        kernel,
        grid_spec=pltpu.PrefetchScalarGridSpec(
            num_scalar_prefetch=1,
            grid=grid,
            in_specs=in_specs,
            out_specs=out_specs,
            scratch_shapes=scratch,
        ),
        out_shape=out_shape,
        compiler_params=pltpu.CompilerParams(vmem_limit_bytes=24 * 1024 * 1024),
        cost_estimate=pl.CostEstimate(flops=flops, bytes_accessed=size, transcendentals=0),
    )


def pack_kernel(place, weights, gain, out):
    out[:LANE, :] = weights[...]
    value = gain[...]
    high = value.astype(BF)
    middle = (value - high.astype(F32)).astype(BF)
    low = (value - high.astype(F32) - middle.astype(F32)).astype(BF)
    row = jnp.concatenate([high, middle, low, jnp.zeros((1, LANE), BF)], axis=1)
    out[LANE:, :] = jnp.broadcast_to(row, (PACK - LANE, KEYS))


def pack(place, weights, gain):
    return call(
        pack_kernel,
        (1,),
        [
            pl.BlockSpec((LANE, KEYS), lambda i, place: (0, 0)),
            pl.BlockSpec((1, LANE), lambda i, place: (0, 0)),
        ],
        pl.BlockSpec((PACK, KEYS), lambda i, place: (0, 0)),
        jax.ShapeDtypeStruct((PACK, KEYS), BF),
        0,
        2 * PACK * KEYS * 2,
    )(place, weights, gain)


def forward_kernel(place, rows_mine, rows_other, packed_mine, packed_other, out, weights):
    rows = out.shape[0] * OWN

    @pl.when(pl.program_id(0) == 0)
    def _():
        weights[:LANE, :] = packed_mine[:LANE, :]
        weights[LANE:, :] = packed_other[:LANE, :]

    left = []
    for block, packed in ((rows_mine, packed_mine), (rows_other, packed_other)):
        pieces = packed[LANE : LANE + 1, :].astype(F32)
        gains = pieces[:, :LANE] + pieces[:, LANE : 2 * LANE] + pieces[:, 2 * LANE : 3 * LANE]
        left.append((block[...].reshape(rows, LANE).astype(F32) * gains).astype(BF))
    total = jnp.dot(jnp.concatenate(left, axis=1), weights[...], preferred_element_type=F32)
    out[...] = total.astype(BF).reshape(out.shape)


def forward(place, fresh, rows_other, packed_mine, packed_other):
    step = 4
    return call(
        forward_kernel,
        (N_T // 2 // step,),
        [
            pl.BlockSpec((step, 1, OWN, LANE), lambda i, place: (i, place[0], 0, 0)),
            pl.BlockSpec((step, OWN, LANE), lambda i, place: (i, 0, 0)),
            pl.BlockSpec((PACK, KEYS), lambda i, place: (0, 0)),
            pl.BlockSpec((PACK, KEYS), lambda i, place: (0, 0)),
        ],
        pl.BlockSpec((step, OWN, KEYS), lambda i, place: (i, 0, 0)),
        jax.ShapeDtypeStruct((N_T // 2, OWN, KEYS), BF),
        2 * TOK // 2 * 2 * LANE * KEYS,
        7 * 1024 * 1024,
        [pltpu.VMEM((2 * LANE, KEYS), BF)],
    )(place, fresh, rows_other, packed_mine, packed_other)


def shards(upstream, stashed, returning, key_cotangent, key_weight, norm_gain, lengths):
    lane = lax.axis_index("ts")
    core = lane % 2
    half = (lane // 2) % 2
    z = lane // 4
    place = core.astype(jnp.int32)[None]
    gain = norm_gain[0]
    weights = key_weight[0]
    fresh = upstream[0]
    saved = stashed[0]

    def by_core(value):
        parts = value.reshape(N_T // 2, 2, OWN, *value.shape[1:])
        return [
            lax.dynamic_index_in_dim(parts, index, 1, keepdims=False).reshape(
                TOK // 2, *value.shape[1:]
            )
            for index in (core, 1 - core)
        ]

    packed = pack(place, weights, norm_gain)
    packed, fresh_rows = lax.optimization_barrier((packed, fresh))
    packed = move(packed, to_previous)

    cot_own = key_cotangent[0]
    cot_half = move(cot_own, to_other_half)
    cot_pair = jnp.stack(
        [jnp.where(half == 0, cot_own, cot_half), jnp.where(half == 0, cot_half, cot_own)]
    )
    lanes = [[q * 4 + j for q in range(N_Z)] for j in range(4)]
    cot_mine = lax.all_gather(cot_pair, "ts", axis=0, axis_index_groups=lanes, tiled=True)
    cot_mine = cot_mine.reshape(TOK // 2, KEYS)

    older_first = move(after(saved[:CUT], cot_half), to_mirror)

    rows = fresh.reshape(N_T // 2, 2, OWN, LANE)
    rows_other = fresh_rows.reshape(N_T // 2, 2, OWN, LANE)
    rows_other = move(
        lax.dynamic_index_in_dim(rows_other, 1 - core, 1, keepdims=False), to_other_core
    )

    fresh_wide = fresh.astype(F32)
    saved_wide = saved.astype(F32)
    fresh_part = jnp.sum(fresh_wide * fresh_wide, axis=1).reshape(N_Z, 2, 2, OWN)
    saved_part = jnp.sum(saved_wide * saved_wide, axis=1).reshape(1, N_T, OWN)
    squares = jnp.concatenate(
        [
            fresh_part.transpose(0, 2, 1, 3).reshape(N_T // 2, 2, OWN).astype(BF),
            jnp.broadcast_to(saved_part.astype(BF), (N_T // 2, N_T, OWN)),
        ],
        axis=1,
    )
    halves = [[q * 4 + h * 2 + c for q in range(N_Z) for c in range(2)] for h in range(2)]
    squares = lax.all_to_all(
        after(squares, packed), "ts", 0, 0, axis_index_groups=halves, tiled=True
    )
    squares_raw = squares
    squares = jnp.sum(squares.astype(F32), axis=0)
    older_sq = [move(squares[2:], to_mirror), move(squares[2:], to_mirror_other_half)]
    fresh_other = move(after(squares[:2], *older_sq), to_other_half)

    older_second = move(after(saved[CUT:], *older_sq), to_mirror)

    early = move(after(returning[0, :SPLIT], *older_sq), to_previous)
    late = returning[0, SPLIT:]

    packed_other = move(packed, to_other_core)
    partial = forward(place, rows, rows_other, packed, packed_other)

    def block(distance):
        return lax.dynamic_slice_in_dim(partial, ((z + distance) % N_Z) * 2, 2, 0)

    up = move(block(4), z_up, (0,))
    down = move(block(4), z_down, (1,))
    base = jnp.zeros((N_T // 2, 2, OWN, LANE), F32)
    up, down, base, late = lax.optimization_barrier(
        (up, down, base, late, squares_raw, older_first, *older_sq)
    )[:4]
    late = move(after(late, early), to_previous)
    up = add(block(3), up)
    down = add(block(-3), down)
    up = move(up, z_up)
    down = move(down, z_down)
    up, down, cot_mine = lax.optimization_barrier((up, down, cot_mine, older_second, early))[:3]

    cots = [cot_mine, move(cot_mine, to_other_core)]
    raw = [
        lax.dot_general(cot, weights, (((1,), (1,)), ((), ())), preferred_element_type=F32)
        for cot in cots
    ]
    up = add(block(2), up)
    down = add(block(-2), down)
    older_first, older_second, *older_sq = lax.optimization_barrier(
        (older_first, older_second, *older_sq, up, down)
    )[:4]
    up = move(up, z_up)
    down = move(down, z_down)
    up, down, raw[0] = lax.optimization_barrier((up, down, raw[0]))
    up = add(block(1), up)
    down = add(block(-1), down)
    up = move(up, z_up)
    down = move(down, z_down)
    older = jnp.concatenate([older_first, older_second], axis=0)
    older_rate = lax.rsqrt((older_sq[0] + older_sq[1]) / WIDTH + eps).reshape(TOK)
    live = (jnp.arange(TOK, dtype=jnp.int32) < lengths[0]).astype(F32)
    scales = by_core(live * older_rate)
    grads = []
    curves = []
    lefts = []
    gain_grad = jnp.zeros((LANE,), F32)
    for cot, product, rows, scale in zip(cots, raw, by_core(older), scales):
        wide = rows.astype(F32)
        grad = scale[:, None] * product
        grads.append(grad)
        curves.append(jnp.sum(grad * (wide * gain).astype(BF).astype(F32), axis=1))
        gain_grad = gain_grad + jnp.sum(grad * wide, axis=0)
        lefts.append(wide * gain * scale[:, None])

    mine = (jnp.arange(2) == core)[None, :, None]
    curve = [part.reshape(N_T // 2, 1, OWN) for part in curves]
    curve = jnp.where(mine, curve[0], curve[1])
    curve = jnp.broadcast_to(curve.reshape(1, N_T, OWN).astype(BF), (N_T, N_T, OWN))
    curve = lax.all_to_all(curve, "ts", 0, 0, tiled=True)
    up, down, fresh_other = lax.optimization_barrier((up, down, fresh_other, curve, late))[:3]
    fresh_rate = lax.rsqrt((squares[:2] + fresh_other) / WIDTH + eps)
    curve = jnp.sum(curve.astype(F32), axis=0).reshape(TOK)
    pull = older_rate * older_rate / WIDTH * curve

    summed = block(0).astype(F32) + up.astype(F32) + down.astype(F32)
    straight = (pick(summed, half) * pick(fresh_rate, half)[:, None]).astype(BF)
    crossed = (pick(summed, 1 - half) * pick(fresh_rate, 1 - half)[:, None]).astype(BF)
    *cots, pull = lax.optimization_barrier((*cots, pull, straight, crossed))[:3]
    straight = move(straight, to_next)
    crossed = move(crossed, to_next_other_half)
    new_keys = (straight.astype(F32) + crossed.astype(F32)).astype(BF)

    weight_total = sum(
        lax.dot_general(
            left.astype(BF), cot, (((0,), (0,)), ((), ())), preferred_element_type=F32
        )
        for left, cot in zip(lefts, cots)
    )
    for index, grad in zip((core, 1 - core), grads):
        base = lax.dynamic_update_index_in_dim(
            base, (gain * grad).reshape(N_T // 2, OWN, LANE), index, 1
        )
    base = base.reshape(TOK, LANE)
    downstream = jnp.concatenate([early, late], axis=0)
    total = downstream.astype(F32) + base - pull[:, None] * older.astype(F32)
    return (
        new_keys[None],
        total.astype(BF)[None],
        weight_total[None],
        gain_grad[None],
    )


def solution(mesh):
    return jax.shard_map(
        shards,
        mesh=mesh,
        in_specs=(
            P("section", None, "ts"),
            P("section", None, "ts"),
            P("section", None, "ts"),
            P("section", "ts", None),
            P("section", "ts", None),
            P("section", "ts"),
            P("section"),
        ),
        out_specs=(
            P("section", "ts", None),
            P("section", None, "ts"),
            P("section", "ts", None),
            P("section", "ts"),
        ),
        check_vma=False,
    )
```

```python
import jax
import jax.numpy as jnp
from jax import lax
from jax.experimental import pallas as pl
from jax.experimental.pallas import tpu as pltpu
from jax.sharding import PartitionSpec as P

eps = 1e-05
BF = jnp.bfloat16
F32 = jnp.float32
N_S = 8
N_T = 32
N_Z = 8
TOK = 4096
OWN = TOK // N_T
WIDTH = 8192
LANE = WIDTH // N_T
KEYS = 1024
PACK = LANE + 16
ORDER = 4
CUT = 3 * TOK // 4
SPLIT = TOK // 4
AXES = ("section", "ts")


def move(value, target, cores=(0, 1)):
    pairs = []
    for s in range(N_S):
        for t in [t for t in range(N_T) if t % 2 in cores]:
            to_s, to_t = target(s, t)
            pairs.append((s * N_T + t, to_s * N_T + to_t))
    return lax.ppermute(value, AXES, pairs)


def to_next(s, t):
    return (s + 1) % N_S, t


def to_previous(s, t):
    return (s - 1) % N_S, t


def to_mirror(s, t):
    return N_S - 1 - s, t


def to_mirror_other_half(s, t):
    return N_S - 1 - s, t ^ 2


def to_other_core(s, t):
    return s, t ^ 1


def to_other_half(s, t):
    return s, t ^ 2


def to_next_other_half(s, t):
    return (s + 1) % N_S, t ^ 2


def z_up(s, t):
    return s, (t + 4) % N_T


def z_down(s, t):
    return s, (t - 4) % N_T


def pick(value, index):
    return lax.dynamic_index_in_dim(value, index, 0, keepdims=False)


def after(value, *others):
    return lax.optimization_barrier((value,) + others)[0]


def add(a, b):
    return (a.astype(F32) + b.astype(F32)).astype(BF)


def call(kernel, grid, in_specs, out_specs, out_shape, flops, size, scratch=()):
    return pl.pallas_call(
        kernel,
        grid_spec=pltpu.PrefetchScalarGridSpec(
            num_scalar_prefetch=1,
            grid=grid,
            in_specs=in_specs,
            out_specs=out_specs,
            scratch_shapes=scratch,
        ),
        out_shape=out_shape,
        compiler_params=pltpu.CompilerParams(vmem_limit_bytes=24 * 1024 * 1024),
        cost_estimate=pl.CostEstimate(flops=flops, bytes_accessed=size, transcendentals=0),
    )


def pack_kernel(place, weights, gain, out):
    out[:LANE, :] = weights[...]
    value = gain[...]
    high = value.astype(BF)
    middle = (value - high.astype(F32)).astype(BF)
    low = (value - high.astype(F32) - middle.astype(F32)).astype(BF)
    row = jnp.concatenate([high, middle, low, jnp.zeros((1, LANE), BF)], axis=1)
    out[LANE:, :] = jnp.broadcast_to(row, (PACK - LANE, KEYS))


def pack(place, weights, gain):
    return call(
        pack_kernel,
        (1,),
        [
            pl.BlockSpec((LANE, KEYS), lambda i, place: (0, 0)),
            pl.BlockSpec((1, LANE), lambda i, place: (0, 0)),
        ],
        pl.BlockSpec((PACK, KEYS), lambda i, place: (0, 0)),
        jax.ShapeDtypeStruct((PACK, KEYS), BF),
        0,
        2 * PACK * KEYS * 2,
    )(place, weights, gain)


def forward_kernel(place, rows_mine, rows_other, packed_mine, packed_other, out, weights):
    rows = out.shape[0] * OWN

    @pl.when(pl.program_id(0) == 0)
    def _():
        weights[:LANE, :] = packed_mine[:LANE, :]
        weights[LANE:, :] = packed_other[:LANE, :]

    left = []
    for block, packed in ((rows_mine, packed_mine), (rows_other, packed_other)):
        pieces = packed[LANE : LANE + 1, :].astype(F32)
        gains = pieces[:, :LANE] + pieces[:, LANE : 2 * LANE] + pieces[:, 2 * LANE : 3 * LANE]
        left.append((block[...].reshape(rows, LANE).astype(F32) * gains).astype(BF))
    total = jnp.dot(jnp.concatenate(left, axis=1), weights[...], preferred_element_type=F32)
    out[...] = total.astype(BF).reshape(out.shape)


def forward(place, fresh, rows_other, packed_mine, packed_other):
    step = 4
    return call(
        forward_kernel,
        (N_T // 2 // step,),
        [
            pl.BlockSpec((step, 1, OWN, LANE), lambda i, place: (i, place[0], 0, 0)),
            pl.BlockSpec((step, OWN, LANE), lambda i, place: (i, 0, 0)),
            pl.BlockSpec((PACK, KEYS), lambda i, place: (0, 0)),
            pl.BlockSpec((PACK, KEYS), lambda i, place: (0, 0)),
        ],
        pl.BlockSpec((step, OWN, KEYS), lambda i, place: (i, 0, 0)),
        jax.ShapeDtypeStruct((N_T // 2, OWN, KEYS), BF),
        2 * TOK // 2 * 2 * LANE * KEYS,
        7 * 1024 * 1024,
        [pltpu.VMEM((2 * LANE, KEYS), BF)],
    )(place, fresh, rows_other, packed_mine, packed_other)


def order_kernel(place, mine, other, gain, out):
    first = place[0] == 0
    token = lax.broadcasted_iota(jnp.int32, (ORDER, OWN, LANE), 0) * 2 * OWN
    token = token + lax.broadcasted_iota(jnp.int32, (ORDER, OWN, LANE), 1)
    token = token + pl.program_id(0) * ORDER * 2 * OWN
    left, right = mine[...] * gain[...], other[...] * gain[...]
    out[:, 0] = jnp.where(token < place[1], jnp.where(first, left, right), 0)
    out[:, 1] = jnp.where(token + OWN < place[1], jnp.where(first, right, left), 0)


def order(place, mine, other, gain):
    half = pl.BlockSpec((ORDER, OWN, LANE), lambda i, place: (i, 0, 0))
    return call(
        order_kernel,
        (N_T // 2 // ORDER,),
        [half, half, pl.BlockSpec((1, LANE), lambda i, place: (0, 0))],
        pl.BlockSpec((ORDER, 2, OWN, LANE), lambda i, place: (i, 0, 0, 0)),
        jax.ShapeDtypeStruct((N_T // 2, 2, OWN, LANE), F32),
        200 * TOK * LANE * KEYS,
        8 * TOK * LANE,
    )(place, mine, other, gain)


def shards(upstream, stashed, returning, key_cotangent, key_weight, norm_gain, lengths):
    lane = lax.axis_index("ts")
    core = lane % 2
    half = (lane // 2) % 2
    z = lane // 4
    place = core.astype(jnp.int32)[None]
    gain = norm_gain[0]
    weights = key_weight[0]
    fresh = upstream[0]
    saved = stashed[0]

    def by_core(value):
        parts = value.reshape(N_T // 2, 2, OWN, *value.shape[1:])
        return [
            lax.dynamic_index_in_dim(parts, index, 1, keepdims=False).reshape(
                TOK // 2, *value.shape[1:]
            )
            for index in (core, 1 - core)
        ]

    packed = pack(place, weights, norm_gain)
    packed, fresh_rows = lax.optimization_barrier((packed, fresh))
    packed = move(packed, to_previous)

    cot_own = key_cotangent[0]
    cot_half = move(cot_own, to_other_half)
    cot_pair = jnp.stack(
        [jnp.where(half == 0, cot_own, cot_half), jnp.where(half == 0, cot_half, cot_own)]
    )
    lanes = [[q * 4 + j for q in range(N_Z)] for j in range(4)]
    cot_mine = lax.all_gather(cot_pair, "ts", axis=0, axis_index_groups=lanes, tiled=True)
    cot_mine = cot_mine.reshape(TOK // 2, KEYS)

    older_first = move(after(saved[:CUT], cot_half), to_mirror)

    rows = fresh.reshape(N_T // 2, 2, OWN, LANE)
    rows_other = fresh_rows.reshape(N_T // 2, 2, OWN, LANE)
    rows_other = move(
        lax.dynamic_index_in_dim(rows_other, 1 - core, 1, keepdims=False), to_other_core
    )

    packed_other = move(packed, to_other_core)
    partial = forward(place, rows, rows_other, packed, packed_other)

    def block(distance):
        return lax.dynamic_slice_in_dim(partial, ((z + distance) % N_Z) * 2, 2, 0)

    far = block(4)

    older_second = move(after(saved[CUT:], partial), to_mirror)
    early = move(after(returning[0, :SPLIT], older_first), to_previous)

    up = move(far, z_up, (0,))
    down = move(far, z_down, (1,))
    fresh_wide = fresh.astype(F32)
    fresh_part = jnp.sum(fresh_wide * fresh_wide, axis=1).astype(BF)
    up, down, late, fresh_part = lax.optimization_barrier(
        (up, down, returning[0, SPLIT:], fresh_part, older_first)
    )[:4]
    late = move(after(late, older_first), to_previous)
    up = move(add(block(3), up), z_up)
    down = move(add(block(-3), down), z_down)
    up, down, cot_mine = lax.optimization_barrier((up, down, cot_mine, older_second, early))[:3]

    cots = [cot_mine, move(cot_mine, to_other_core)]
    def times_weights(cot):
        return lax.dot_general(cot, weights, (((1,), (1,)), ((), ())), preferred_element_type=F32)

    raw = [times_weights(cots[0])]
    up = add(block(2), up)
    down = add(block(-2), down)
    older_first, older_second = lax.optimization_barrier((older_first, older_second, up, down))[:2]
    up = move(up, z_up)
    down = move(down, z_down)
    up, down, raw[0] = lax.optimization_barrier((up, down, raw[0]))
    up = add(block(1), up)
    down = add(block(-1), down)
    cots[1] = after(cots[1], up, down)
    raw.append(times_weights(cots[1]))
    up = move(up, z_up)
    down = move(down, z_down)

    older = jnp.concatenate([older_first, older_second], axis=0)
    wide = older.astype(F32)
    part_sq = jnp.sum(wide * wide, axis=1).astype(BF)
    part_rate = lax.rsqrt(part_sq.astype(F32) / LANE + eps)
    mine = (jnp.arange(2) == core)[None, :, None]
    curve = [
        jnp.sum(
            (scale[:, None] * product) * (rows.astype(F32) * gain).astype(BF).astype(F32), axis=1
        ).reshape(N_T // 2, 1, OWN)
        for product, rows, scale in zip(raw, by_core(older), by_core(part_rate))
    ]
    curve = jnp.where(mine, curve[0], curve[1]).reshape(1, N_T, OWN).astype(BF)
    fresh_part = fresh_part.reshape(N_Z, 2, 2, OWN)
    sent = jnp.concatenate(
        [
            jnp.broadcast_to(curve, (N_T, N_T, OWN)),
            jnp.broadcast_to(part_sq.reshape(1, N_T, OWN), (N_T, N_T, OWN)),
            fresh_part.reshape(N_T, 1, OWN),
            fresh_part[:, ::-1].reshape(N_T, 1, OWN),
        ],
        axis=1,
    )
    ordered = order(
        jnp.concatenate([place, lengths]),
        *[product.reshape(N_T // 2, OWN, LANE) for product in raw],
        norm_gain,
    )
    got = lax.all_to_all(sent, "ts", 0, 0, tiled=True)
    up, down = lax.optimization_barrier((up, down, got, late))[:2]
    got, ordered = lax.optimization_barrier((got, ordered))
    got = got.astype(F32)
    live = (jnp.arange(TOK, dtype=jnp.int32) < lengths[0]).reshape(N_T, OWN)
    older_rate = lax.rsqrt(jnp.sum(got[:, N_T : 2 * N_T], axis=0) / WIDTH + eps)
    curve = jnp.sum(
        got[:, :N_T] * (older_rate * jnp.sqrt(got[:, N_T : 2 * N_T] / LANE + eps)), axis=0
    )
    pull = jnp.where(live, older_rate * older_rate / WIDTH * curve, 0).reshape(TOK)
    scale = jnp.where(live, older_rate, 0).reshape(TOK)
    fresh_rate = lax.rsqrt(jnp.sum(got[:, 2 * N_T :], axis=0) / WIDTH + eps)

    summed = block(0).astype(F32) + up.astype(F32) + down.astype(F32)
    straight = (pick(summed, half) * fresh_rate[0][:, None]).astype(BF)
    crossed = (pick(summed, 1 - half) * fresh_rate[1][:, None]).astype(BF)
    *cots, pull, scale = lax.optimization_barrier((*cots, pull, scale, straight, crossed))[:4]
    straight = move(straight, to_next)
    crossed = move(crossed, to_next_other_half)
    new_keys = (straight.astype(F32) + crossed.astype(F32)).astype(BF)

    weight_total = sum(
        lax.dot_general(
            (rows.astype(F32) * gain * row_scale[:, None]).astype(BF),
            cot,
            (((0,), (0,)), ((), ())),
            preferred_element_type=F32,
        )
        for cot, rows, row_scale in zip(cots, by_core(older), by_core(scale))
    )
    gain_grad = jnp.sum(weights.astype(F32) * weight_total, axis=1) / gain
    downstream = jnp.concatenate([early, late], axis=0)
    total = (
        downstream.astype(F32)
        + scale[:, None] * ordered.reshape(TOK, LANE)
        - pull[:, None] * wide
    )
    return (
        new_keys[None],
        total.astype(BF)[None],
        weight_total[None],
        gain_grad[None],
    )


def solution(mesh):
    return jax.shard_map(
        shards,
        mesh=mesh,
        in_specs=(
            P("section", None, "ts"),
            P("section", None, "ts"),
            P("section", None, "ts"),
            P("section", "ts", None),
            P("section", "ts", None),
            P("section", "ts"),
            P("section"),
        ),
        out_specs=(
            P("section", "ts", None),
            P("section", None, "ts"),
            P("section", "ts", None),
            P("section", "ts"),
        ),
        check_vma=False,
    )
```

```python
import jax
import jax.numpy as jnp
from jax import lax
from jax.experimental import pallas as pl
from jax.experimental.pallas import tpu as pltpu
from jax.sharding import PartitionSpec as P

eps = 1e-05
BF = jnp.bfloat16
F32 = jnp.float32
N_S = 8
N_T = 32
N_Z = 8
TOK = 4096
OWN = TOK // N_T
WIDTH = 8192
LANE = WIDTH // N_T
KEYS = 1024
PACK = LANE + 16
ORDER = 4
CUT = TOK // 2
SPLIT = 3 * TOK // 4
AXES = ("section", "ts")


def move(value, target, cores=(0, 1)):
    pairs = []
    for s in range(N_S):
        for t in [t for t in range(N_T) if t % 2 in cores]:
            to_s, to_t = target(s, t)
            pairs.append((s * N_T + t, to_s * N_T + to_t))
    return lax.ppermute(value, AXES, pairs)


def to_next(s, t):
    return (s + 1) % N_S, t


def to_previous(s, t):
    return (s - 1) % N_S, t


def to_mirror(s, t):
    return N_S - 1 - s, t


def to_mirror_other_half(s, t):
    return N_S - 1 - s, t ^ 2


def to_other_core(s, t):
    return s, t ^ 1


def to_other_half(s, t):
    return s, t ^ 2


def to_next_other_half(s, t):
    return (s + 1) % N_S, t ^ 2


def z_up(s, t):
    return s, (t + 4) % N_T


def z_down(s, t):
    return s, (t - 4) % N_T


def pick(value, index):
    return lax.dynamic_index_in_dim(value, index, 0, keepdims=False)


def after(value, *others):
    return lax.optimization_barrier((value,) + others)[0]


def add(a, b):
    return (a.astype(F32) + b.astype(F32)).astype(BF)


def call(kernel, grid, in_specs, out_specs, out_shape, flops, size, scratch=()):
    return pl.pallas_call(
        kernel,
        grid_spec=pltpu.PrefetchScalarGridSpec(
            num_scalar_prefetch=1,
            grid=grid,
            in_specs=in_specs,
            out_specs=out_specs,
            scratch_shapes=scratch,
        ),
        out_shape=out_shape,
        compiler_params=pltpu.CompilerParams(vmem_limit_bytes=24 * 1024 * 1024),
        cost_estimate=pl.CostEstimate(flops=flops, bytes_accessed=size, transcendentals=0),
    )


def pack_kernel(place, weights, gain, out):
    out[:LANE, :] = weights[...]
    value = gain[...]
    high = value.astype(BF)
    middle = (value - high.astype(F32)).astype(BF)
    low = (value - high.astype(F32) - middle.astype(F32)).astype(BF)
    row = jnp.concatenate([high, middle, low, jnp.zeros((1, LANE), BF)], axis=1)
    out[LANE:, :] = jnp.broadcast_to(row, (PACK - LANE, KEYS))


def pack(place, weights, gain):
    return call(
        pack_kernel,
        (1,),
        [
            pl.BlockSpec((LANE, KEYS), lambda i, place: (0, 0)),
            pl.BlockSpec((1, LANE), lambda i, place: (0, 0)),
        ],
        pl.BlockSpec((PACK, KEYS), lambda i, place: (0, 0)),
        jax.ShapeDtypeStruct((PACK, KEYS), BF),
        0,
        2 * PACK * KEYS * 2,
    )(place, weights, gain)


def forward_kernel(place, rows_mine, rows_other, packed_mine, packed_other, out, weights):
    rows = out.shape[0] * OWN

    @pl.when(pl.program_id(0) == 0)
    def _():
        weights[:LANE, :] = packed_mine[:LANE, :]
        weights[LANE:, :] = packed_other[:LANE, :]

    left = []
    for block, packed in ((rows_mine, packed_mine), (rows_other, packed_other)):
        pieces = packed[LANE : LANE + 1, :].astype(F32)
        gains = pieces[:, :LANE] + pieces[:, LANE : 2 * LANE] + pieces[:, 2 * LANE : 3 * LANE]
        left.append((block[...].reshape(rows, LANE).astype(F32) * gains).astype(BF))
    total = jnp.dot(jnp.concatenate(left, axis=1), weights[...], preferred_element_type=F32)
    out[...] = total.astype(BF).reshape(out.shape)


def forward(place, fresh, rows_other, packed_mine, packed_other):
    step = 4
    return call(
        forward_kernel,
        (N_T // 2 // step,),
        [
            pl.BlockSpec((step, 1, OWN, LANE), lambda i, place: (i, place[0], 0, 0)),
            pl.BlockSpec((step, OWN, LANE), lambda i, place: (i, 0, 0)),
            pl.BlockSpec((PACK, KEYS), lambda i, place: (0, 0)),
            pl.BlockSpec((PACK, KEYS), lambda i, place: (0, 0)),
        ],
        pl.BlockSpec((step, OWN, KEYS), lambda i, place: (i, 0, 0)),
        jax.ShapeDtypeStruct((N_T // 2, OWN, KEYS), BF),
        2 * TOK // 2 * 2 * LANE * KEYS,
        7 * 1024 * 1024,
        [pltpu.VMEM((2 * LANE, KEYS), BF)],
    )(place, fresh, rows_other, packed_mine, packed_other)


def order_kernel(place, mine, other, gain, out):
    first = place[0] == 0
    token = lax.broadcasted_iota(jnp.int32, (ORDER, OWN, LANE), 0) * 2 * OWN
    token = token + lax.broadcasted_iota(jnp.int32, (ORDER, OWN, LANE), 1)
    token = token + pl.program_id(0) * ORDER * 2 * OWN
    left, right = mine[...] * gain[...], other[...] * gain[...]
    out[:, 0] = jnp.where(token < place[1], jnp.where(first, left, right), 0)
    out[:, 1] = jnp.where(token + OWN < place[1], jnp.where(first, right, left), 0)


def order(place, mine, other, gain):
    half = pl.BlockSpec((ORDER, OWN, LANE), lambda i, place: (i, 0, 0))
    return call(
        order_kernel,
        (N_T // 2 // ORDER,),
        [half, half, pl.BlockSpec((1, LANE), lambda i, place: (0, 0))],
        pl.BlockSpec((ORDER, 2, OWN, LANE), lambda i, place: (i, 0, 0, 0)),
        jax.ShapeDtypeStruct((N_T // 2, 2, OWN, LANE), F32),
        200 * TOK * LANE * KEYS,
        8 * TOK * LANE,
    )(place, mine, other, gain)


def shards(upstream, stashed, returning, key_cotangent, key_weight, norm_gain, lengths):
    lane = lax.axis_index("ts")
    core = lane % 2
    half = (lane // 2) % 2
    z = lane // 4
    place = core.astype(jnp.int32)[None]
    gain = norm_gain[0]
    weights = key_weight[0]
    fresh = upstream[0]
    saved = stashed[0]

    def by_core(value):
        parts = value.reshape(N_T // 2, 2, OWN, *value.shape[1:])
        return [
            lax.dynamic_index_in_dim(parts, index, 1, keepdims=False).reshape(
                TOK // 2, *value.shape[1:]
            )
            for index in (core, 1 - core)
        ]

    packed = pack(place, weights, norm_gain)
    packed, fresh_rows = lax.optimization_barrier((packed, fresh))
    packed = move(packed, to_previous)

    cot_own = key_cotangent[0]
    cot_half = move(cot_own, to_other_half)
    cot_pair = jnp.stack(
        [jnp.where(half == 0, cot_own, cot_half), jnp.where(half == 0, cot_half, cot_own)]
    )
    lanes = [[q * 4 + j for q in range(N_Z)] for j in range(4)]
    cot_mine = lax.all_gather(cot_pair, "ts", axis=0, axis_index_groups=lanes, tiled=True)
    cot_mine = cot_mine.reshape(TOK // 2, KEYS)

    older_first = move(after(saved[:CUT], cot_half), to_mirror)

    rows = fresh.reshape(N_T // 2, 2, OWN, LANE)
    rows_other = fresh_rows.reshape(N_T // 2, 2, OWN, LANE)
    rows_other = move(
        lax.dynamic_index_in_dim(rows_other, 1 - core, 1, keepdims=False), to_other_core
    )

    packed_other = move(packed, to_other_core)
    partial = forward(place, rows, rows_other, packed, packed_other)

    def block(distance):
        return lax.dynamic_slice_in_dim(partial, ((z + distance) % N_Z) * 2, 2, 0)

    far = block(4)

    older_second = move(after(saved[CUT:], partial), to_mirror)
    early = move(after(returning[0, :SPLIT], older_first), to_previous)

    up = move(far, z_up, (0,))
    down = move(far, z_down, (1,))
    fresh_wide = fresh.astype(F32)
    fresh_part = jnp.sum(fresh_wide * fresh_wide, axis=1)
    up, down, late, fresh_part = lax.optimization_barrier(
        (up, down, returning[0, SPLIT:], fresh_part, older_first)
    )[:4]
    up = move(add(block(3), up), z_up)
    down = move(add(block(-3), down), z_down)
    up, down, cot_mine = lax.optimization_barrier((up, down, cot_mine, older_second))[:3]

    cots = [cot_mine, move(cot_mine, to_other_core)]
    def times_weights(cot):
        return lax.dot_general(cot, weights, (((1,), (1,)), ((), ())), preferred_element_type=F32)

    raw = [times_weights(cots[0])]
    up = add(block(2), up)
    down = add(block(-2), down)
    older_first, older_second = lax.optimization_barrier((older_first, older_second, up, down))[:2]
    up = move(up, z_up)
    down = move(down, z_down)
    up, down, raw[0] = lax.optimization_barrier((up, down, raw[0]))
    up = add(block(1), up)
    down = add(block(-1), down)
    cots[1] = after(cots[1], up, down)
    raw.append(times_weights(cots[1]))
    up = move(up, z_up)
    down = move(down, z_down)

    older = jnp.concatenate([older_first, older_second], axis=0)
    wide = older.astype(F32)
    part_sq = jnp.sum(wide * wide, axis=1)
    part_rate = lax.rsqrt(part_sq / LANE + eps)
    mine = (jnp.arange(2) == core)[None, :, None]
    curve = [
        jnp.sum(
            (scale[:, None] * product) * (rows.astype(F32) * gain).astype(BF).astype(F32), axis=1
        ).reshape(N_T // 2, 1, OWN)
        for product, rows, scale in zip(raw, by_core(older), by_core(part_rate))
    ]
    curve = jnp.where(mine, curve[0], curve[1])
    fresh_part = fresh_part.reshape(N_Z, 2, 2, OWN)
    sent = [curve, part_sq, fresh_part, fresh_part[:, ::-1]]
    sent = jnp.concatenate([value.reshape(N_T, 1, OWN) for value in sent], axis=1)
    ordered = order(
        jnp.concatenate([place, lengths]),
        *[product.reshape(N_T // 2, OWN, LANE) for product in raw],
        norm_gain,
    )
    got = lax.all_to_all(sent, "ts", 0, 0, tiled=True)
    late = move(after(late, ordered), to_previous)
    up, down = lax.optimization_barrier((up, down, got, early, late))[:2]
    got, ordered = lax.optimization_barrier((got, ordered))

    live = lane * OWN + jnp.arange(OWN, dtype=jnp.int32) < lengths[0]
    own_rate = lax.rsqrt(jnp.sum(got[:, 1], axis=0) / WIDTH + eps)
    own_curve = jnp.sum(got[:, 0] * (own_rate * jnp.sqrt(got[:, 1] / LANE + eps)), axis=0)
    factors = jnp.stack(
        [jnp.where(live, own_rate, 0), jnp.where(live, own_rate * own_rate / WIDTH * own_curve, 0)]
    )
    factors = jnp.broadcast_to(factors[None], (N_T, 2, OWN))
    factors = lax.all_to_all(factors, "ts", 0, 0, tiled=True)
    fresh_rate = lax.rsqrt(jnp.sum(got[:, 2:], axis=0) / WIDTH + eps)

    summed = block(0).astype(F32) + up.astype(F32) + down.astype(F32)
    straight = (pick(summed, half) * fresh_rate[0][:, None]).astype(BF)
    crossed = (pick(summed, 1 - half) * fresh_rate[1][:, None]).astype(BF)
    *cots, factors = lax.optimization_barrier((*cots, factors, straight, crossed))[:3]
    scale, pull = factors[:, 0].reshape(TOK), factors[:, 1].reshape(TOK)
    straight = move(straight, to_next)
    crossed = move(crossed, to_next_other_half)
    new_keys = (straight.astype(F32) + crossed.astype(F32)).astype(BF)

    weight_total = sum(
        lax.dot_general(
            (rows.astype(F32) * gain * row_scale[:, None]).astype(BF),
            cot,
            (((0,), (0,)), ((), ())),
            preferred_element_type=F32,
        )
        for cot, rows, row_scale in zip(cots, by_core(older), by_core(scale))
    )
    gain_grad = jnp.sum(weights.astype(F32) * weight_total, axis=1) / gain
    downstream = jnp.concatenate([early, late], axis=0)
    total = (
        downstream.astype(F32)
        + scale[:, None] * ordered.reshape(TOK, LANE)
        - pull[:, None] * wide
    )
    return (
        new_keys[None],
        total.astype(BF)[None],
        weight_total[None],
        gain_grad[None],
    )


def solution(mesh):
    return jax.shard_map(
        shards,
        mesh=mesh,
        in_specs=(
            P("section", None, "ts"),
            P("section", None, "ts"),
            P("section", None, "ts"),
            P("section", "ts", None),
            P("section", "ts", None),
            P("section", "ts"),
            P("section"),
        ),
        out_specs=(
            P("section", "ts", None),
            P("section", None, "ts"),
            P("section", "ts", None),
            P("section", "ts"),
        ),
        check_vma=False,
    )
```

```python
import jax
import jax.numpy as jnp
from jax import lax
from jax.experimental import pallas as pl
from jax.experimental.pallas import tpu as pltpu
from jax.sharding import PartitionSpec as P

eps = 1e-05
BF = jnp.bfloat16
F32 = jnp.float32
N_S = 8
N_T = 32
N_Z = 8
TOK = 4096
OWN = TOK // N_T
WIDTH = 8192
LANE = WIDTH // N_T
KEYS = 1024
PACK = LANE + 16
ORDER = 4
CUT = 3 * TOK // 4
SPLIT = 3 * TOK // 16
AXES = ("section", "ts")


def move(value, target, cores=(0, 1)):
    pairs = []
    for s in range(N_S):
        for t in [t for t in range(N_T) if t % 2 in cores]:
            to_s, to_t = target(s, t)
            pairs.append((s * N_T + t, to_s * N_T + to_t))
    return lax.ppermute(value, AXES, pairs)


def to_next(s, t):
    return (s + 1) % N_S, t


def to_previous(s, t):
    return (s - 1) % N_S, t


def to_mirror(s, t):
    return N_S - 1 - s, t


def to_mirror_other_half(s, t):
    return N_S - 1 - s, t ^ 2


def to_other_core(s, t):
    return s, t ^ 1


def to_other_half(s, t):
    return s, t ^ 2


def to_next_other_half(s, t):
    return (s + 1) % N_S, t ^ 2


def z_up(s, t):
    return s, (t + 4) % N_T


def z_down(s, t):
    return s, (t - 4) % N_T


def pick(value, index):
    return lax.dynamic_index_in_dim(value, index, 0, keepdims=False)


def after(value, *others):
    return lax.optimization_barrier((value,) + others)[0]


def add(a, b):
    return (a.astype(F32) + b.astype(F32)).astype(BF)


def call(kernel, grid, in_specs, out_specs, out_shape, flops, size, scratch=()):
    return pl.pallas_call(
        kernel,
        grid_spec=pltpu.PrefetchScalarGridSpec(
            num_scalar_prefetch=1,
            grid=grid,
            in_specs=in_specs,
            out_specs=out_specs,
            scratch_shapes=scratch,
        ),
        out_shape=out_shape,
        compiler_params=pltpu.CompilerParams(vmem_limit_bytes=24 * 1024 * 1024),
        cost_estimate=pl.CostEstimate(flops=flops, bytes_accessed=size, transcendentals=0),
    )


def pack_kernel(place, weights, gain, out):
    out[:LANE, :] = weights[...]
    value = gain[...]
    high = value.astype(BF)
    middle = (value - high.astype(F32)).astype(BF)
    low = (value - high.astype(F32) - middle.astype(F32)).astype(BF)
    row = jnp.concatenate([high, middle, low, jnp.zeros((1, LANE), BF)], axis=1)
    out[LANE:, :] = jnp.broadcast_to(row, (PACK - LANE, KEYS))


def pack(place, weights, gain):
    return call(
        pack_kernel,
        (1,),
        [
            pl.BlockSpec((LANE, KEYS), lambda i, place: (0, 0)),
            pl.BlockSpec((1, LANE), lambda i, place: (0, 0)),
        ],
        pl.BlockSpec((PACK, KEYS), lambda i, place: (0, 0)),
        jax.ShapeDtypeStruct((PACK, KEYS), BF),
        0,
        2 * PACK * KEYS * 2,
    )(place, weights, gain)


def forward_kernel(place, rows_mine, rows_other, packed_mine, packed_other, out, weights):
    rows = out.shape[0] * OWN

    @pl.when(pl.program_id(0) == 0)
    def _():
        weights[:LANE, :] = packed_mine[:LANE, :]
        weights[LANE:, :] = packed_other[:LANE, :]

    left = []
    for block, packed in ((rows_mine, packed_mine), (rows_other, packed_other)):
        pieces = packed[LANE : LANE + 1, :].astype(F32)
        gains = pieces[:, :LANE] + pieces[:, LANE : 2 * LANE] + pieces[:, 2 * LANE : 3 * LANE]
        left.append((block[...].reshape(rows, LANE).astype(F32) * gains).astype(BF))
    total = jnp.dot(jnp.concatenate(left, axis=1), weights[...], preferred_element_type=F32)
    out[...] = total.astype(BF).reshape(out.shape)


def forward(place, fresh, rows_other, packed_mine, packed_other):
    step = 4
    return call(
        forward_kernel,
        (N_T // 2 // step,),
        [
            pl.BlockSpec((step, 1, OWN, LANE), lambda i, place: (i, place[0], 0, 0)),
            pl.BlockSpec((step, OWN, LANE), lambda i, place: (i, 0, 0)),
            pl.BlockSpec((PACK, KEYS), lambda i, place: (0, 0)),
            pl.BlockSpec((PACK, KEYS), lambda i, place: (0, 0)),
        ],
        pl.BlockSpec((step, OWN, KEYS), lambda i, place: (i, 0, 0)),
        jax.ShapeDtypeStruct((N_T // 2, OWN, KEYS), BF),
        2 * TOK // 2 * 2 * LANE * KEYS,
        7 * 1024 * 1024,
        [pltpu.VMEM((2 * LANE, KEYS), BF)],
    )(place, fresh, rows_other, packed_mine, packed_other)


def order_kernel(place, mine, other, out):
    first = place[0] == 0
    out[:, 0] = jnp.where(first, mine[...], other[...])
    out[:, 1] = jnp.where(first, other[...], mine[...])


def order(place, mine, other):
    half = pl.BlockSpec((ORDER, OWN, LANE), lambda i, place: (i, 0, 0))
    return call(
        order_kernel,
        (N_T // 2 // ORDER,),
        [half, half],
        pl.BlockSpec((ORDER, 2, OWN, LANE), lambda i, place: (i, 0, 0, 0)),
        jax.ShapeDtypeStruct((N_T // 2, 2, OWN, LANE), F32),
        200 * TOK * LANE * KEYS,
        8 * TOK * LANE,
    )(place, mine, other)


def shards(upstream, stashed, returning, key_cotangent, key_weight, norm_gain, lengths):
    lane = lax.axis_index("ts")
    core = lane % 2
    half = (lane // 2) % 2
    z = lane // 4
    place = core.astype(jnp.int32)[None]
    gain = norm_gain[0]
    weights = key_weight[0]
    fresh = upstream[0]
    saved = stashed[0]

    def by_core(value):
        parts = value.reshape(N_T // 2, 2, OWN, *value.shape[1:])
        return [
            lax.dynamic_index_in_dim(parts, index, 1, keepdims=False).reshape(
                TOK // 2, *value.shape[1:]
            )
            for index in (core, 1 - core)
        ]

    packed = pack(place, weights, norm_gain)
    packed, fresh_rows = lax.optimization_barrier((packed, fresh))
    packed = move(packed, to_previous)

    cot_own = key_cotangent[0]
    cot_half = move(cot_own, to_other_half)
    cot_pair = jnp.stack(
        [jnp.where(half == 0, cot_own, cot_half), jnp.where(half == 0, cot_half, cot_own)]
    )
    lanes = [[q * 4 + j for q in range(N_Z)] for j in range(4)]
    cot_mine = lax.all_gather(cot_pair, "ts", axis=0, axis_index_groups=lanes, tiled=True)
    cot_mine = cot_mine.reshape(TOK // 2, KEYS)

    older_first = move(after(saved[:CUT], cot_half), to_mirror)

    rows = fresh.reshape(N_T // 2, 2, OWN, LANE)
    rows_other = fresh_rows.reshape(N_T // 2, 2, OWN, LANE)
    rows_other = move(
        lax.dynamic_index_in_dim(rows_other, 1 - core, 1, keepdims=False), to_other_core
    )

    fresh_wide = fresh.astype(F32)
    saved_wide = saved.astype(F32)
    fresh_part = jnp.sum(fresh_wide * fresh_wide, axis=1).reshape(N_Z, 2, 2, OWN)
    saved_part = jnp.sum(saved_wide * saved_wide, axis=1).reshape(1, N_T, OWN)
    squares = jnp.concatenate(
        [
            fresh_part.transpose(0, 2, 1, 3).reshape(N_T // 2, 2, OWN).astype(BF),
            jnp.broadcast_to(saved_part.astype(BF), (N_T // 2, N_T, OWN)),
        ],
        axis=1,
    )
    halves = [[q * 4 + h * 2 + c for q in range(N_Z) for c in range(2)] for h in range(2)]
    squares = lax.all_to_all(
        after(squares, packed), "ts", 0, 0, axis_index_groups=halves, tiled=True
    )
    squares_raw = squares
    squares = jnp.sum(squares.astype(F32), axis=0)
    older_sq = [move(squares[2:], to_mirror), move(squares[2:], to_mirror_other_half)]
    fresh_other = move(after(squares[:2], *older_sq), to_other_half)

    older_second = move(after(saved[CUT:], *older_sq), to_mirror)

    early = move(after(returning[0, :SPLIT], *older_sq), to_previous)
    late = returning[0, SPLIT:]

    packed_other = move(packed, to_other_core)
    partial = forward(place, rows, rows_other, packed, packed_other)

    def block(distance):
        return lax.dynamic_slice_in_dim(partial, ((z + distance) % N_Z) * 2, 2, 0)

    up = move(block(4), z_up, (0,))
    down = move(block(4), z_down, (1,))
    up, down, late = lax.optimization_barrier(
        (up, down, late, squares_raw, older_first, *older_sq)
    )[:3]
    late = move(after(late, early), to_previous)
    up = add(block(3), up)
    down = add(block(-3), down)
    up = move(up, z_up)
    down = move(down, z_down)
    up, down, cot_mine, fresh_other = lax.optimization_barrier(
        (up, down, cot_mine, fresh_other, older_second, early)
    )[:4]

    cots = [cot_mine, move(cot_mine, to_other_core)]
    raw = [
        lax.dot_general(cot, weights, (((1,), (1,)), ((), ())), preferred_element_type=F32)
        for cot in cots
    ]
    up = add(block(2), up)
    down = add(block(-2), down)
    older_first, older_second, *older_sq = lax.optimization_barrier(
        (older_first, older_second, *older_sq, up, down)
    )[:4]
    up = move(up, z_up)
    down = move(down, z_down)
    up, down, raw[0] = lax.optimization_barrier((up, down, raw[0]))
    up = add(block(1), up)
    down = add(block(-1), down)
    up = move(up, z_up)
    down = move(down, z_down)
    older = jnp.concatenate([older_first, older_second], axis=0)
    older_rate = lax.rsqrt((older_sq[0] + older_sq[1]) / WIDTH + eps).reshape(TOK)
    live = (jnp.arange(TOK, dtype=jnp.int32) < lengths[0]).astype(F32)
    scales = by_core(live * older_rate)
    grads = []
    curves = []
    lefts = []
    gain_grad = jnp.zeros((LANE,), F32)
    for cot, product, rows, scale in zip(cots, raw, by_core(older), scales):
        wide = rows.astype(F32)
        grad = scale[:, None] * product
        grads.append(grad)
        curves.append(jnp.sum(grad * (wide * gain).astype(BF).astype(F32), axis=1))
        gain_grad = gain_grad + jnp.sum(grad * wide, axis=0)
        lefts.append(wide * gain * scale[:, None])

    mine = (jnp.arange(2) == core)[None, :, None]
    curve = [part.reshape(N_T // 2, 1, OWN) for part in curves]
    curve = jnp.where(mine, curve[0], curve[1])
    curve = jnp.broadcast_to(curve.reshape(1, N_T, OWN).astype(BF), (N_T, N_T, OWN))
    base = order(
        place, *[(gain * grad).reshape(N_T // 2, OWN, LANE) for grad in grads]
    ).reshape(TOK, LANE)
    curve = lax.all_to_all(curve, "ts", 0, 0, tiled=True)
    up, down, base = lax.optimization_barrier((up, down, base, late))[:3]
    fresh_rate = lax.rsqrt((squares[:2] + fresh_other) / WIDTH + eps)

    summed = block(0).astype(F32) + up.astype(F32) + down.astype(F32)
    straight = (pick(summed, half) * pick(fresh_rate, half)[:, None]).astype(BF)
    crossed = (pick(summed, 1 - half) * pick(fresh_rate, 1 - half)[:, None]).astype(BF)
    cots = lax.optimization_barrier((*cots, straight, crossed))[:2]
    straight = move(straight, to_next)
    crossed = move(crossed, to_next_other_half)
    new_keys = (straight.astype(F32) + crossed.astype(F32)).astype(BF)

    weight_total = sum(
        lax.dot_general(
            left.astype(BF), cot, (((0,), (0,)), ((), ())), preferred_element_type=F32
        )
        for left, cot in zip(lefts, cots)
    )
    curve, base, weight_total = lax.optimization_barrier((curve, base, weight_total))
    curve = jnp.sum(curve.astype(F32), axis=0).reshape(TOK)
    pull = older_rate * older_rate / WIDTH * curve
    downstream = jnp.concatenate([early, late], axis=0)
    total = downstream.astype(F32) + base - pull[:, None] * older.astype(F32)
    return (
        new_keys[None],
        total.astype(BF)[None],
        weight_total[None],
        gain_grad[None],
    )


def solution(mesh):
    return jax.shard_map(
        shards,
        mesh=mesh,
        in_specs=(
            P("section", None, "ts"),
            P("section", None, "ts"),
            P("section", None, "ts"),
            P("section", "ts", None),
            P("section", "ts", None),
            P("section", "ts"),
            P("section"),
        ),
        out_specs=(
            P("section", "ts", None),
            P("section", None, "ts"),
            P("section", "ts", None),
            P("section", "ts"),
        ),
        check_vma=False,
    )
```

```python
import jax
import jax.numpy as jnp
from jax import lax
from jax.experimental import pallas as pl
from jax.experimental.pallas import tpu as pltpu
from jax.sharding import PartitionSpec as P

eps = 1e-05
BF = jnp.bfloat16
F32 = jnp.float32
N_S = 8
N_T = 32
N_Z = 8
TOK = 4096
OWN = TOK // N_T
WIDTH = 8192
LANE = WIDTH // N_T
KEYS = 1024
PACK = LANE + 16
CUT = TOK // 2
AXES = ("section", "ts")


def move(value, target, cores=(0, 1)):
    pairs = []
    for s in range(N_S):
        for t in [t for t in range(N_T) if t % 2 in cores]:
            to_s, to_t = target(s, t)
            pairs.append((s * N_T + t, to_s * N_T + to_t))
    return lax.ppermute(value, AXES, pairs)


def to_next(s, t):
    return (s + 1) % N_S, t


def to_previous(s, t):
    return (s - 1) % N_S, t


def to_mirror(s, t):
    return N_S - 1 - s, t


def to_mirror_other_half(s, t):
    return N_S - 1 - s, t ^ 2


def to_other_core(s, t):
    return s, t ^ 1


def to_other_half(s, t):
    return s, t ^ 2


def to_next_other_half(s, t):
    return (s + 1) % N_S, t ^ 2


def z_up(s, t):
    return s, (t + 4) % N_T


def z_down(s, t):
    return s, (t - 4) % N_T


def pick(value, index):
    return lax.dynamic_index_in_dim(value, index, 0, keepdims=False)


def after(value, *others):
    return lax.optimization_barrier((value,) + others)[0]


def add(a, b):
    return (a.astype(F32) + b.astype(F32)).astype(BF)


def call(kernel, grid, in_specs, out_specs, out_shape, flops, size, scratch=()):
    return pl.pallas_call(
        kernel,
        grid_spec=pltpu.PrefetchScalarGridSpec(
            num_scalar_prefetch=1,
            grid=grid,
            in_specs=in_specs,
            out_specs=out_specs,
            scratch_shapes=scratch,
        ),
        out_shape=out_shape,
        compiler_params=pltpu.CompilerParams(vmem_limit_bytes=24 * 1024 * 1024),
        cost_estimate=pl.CostEstimate(flops=flops, bytes_accessed=size, transcendentals=0),
    )


def pack_kernel(place, weights, gain, out):
    out[:LANE, :] = weights[...]
    value = gain[...]
    high = value.astype(BF)
    middle = (value - high.astype(F32)).astype(BF)
    low = (value - high.astype(F32) - middle.astype(F32)).astype(BF)
    row = jnp.concatenate([high, middle, low, jnp.zeros((1, LANE), BF)], axis=1)
    out[LANE:, :] = jnp.broadcast_to(row, (PACK - LANE, KEYS))


def pack(place, weights, gain):
    return call(
        pack_kernel,
        (1,),
        [
            pl.BlockSpec((LANE, KEYS), lambda i, place: (0, 0)),
            pl.BlockSpec((1, LANE), lambda i, place: (0, 0)),
        ],
        pl.BlockSpec((PACK, KEYS), lambda i, place: (0, 0)),
        jax.ShapeDtypeStruct((PACK, KEYS), BF),
        0,
        2 * PACK * KEYS * 2,
    )(place, weights, gain)


def forward_kernel(place, rows_mine, rows_other, packed_mine, packed_other, out, weights):
    rows = out.shape[0] * OWN

    @pl.when(pl.program_id(0) == 0)
    def _():
        weights[:LANE, :] = packed_mine[:LANE, :]
        weights[LANE:, :] = packed_other[:LANE, :]

    left = []
    for block, packed in ((rows_mine, packed_mine), (rows_other, packed_other)):
        pieces = packed[LANE : LANE + 1, :].astype(F32)
        gains = pieces[:, :LANE] + pieces[:, LANE : 2 * LANE] + pieces[:, 2 * LANE : 3 * LANE]
        left.append((block[...].reshape(rows, LANE).astype(F32) * gains).astype(BF))
    total = jnp.dot(jnp.concatenate(left, axis=1), weights[...], preferred_element_type=F32)
    out[...] = total.astype(BF).reshape(out.shape)


def forward(place, fresh, rows_other, packed_mine, packed_other):
    step = 4
    return call(
        forward_kernel,
        (N_T // 2 // step,),
        [
            pl.BlockSpec((step, 1, OWN, LANE), lambda i, place: (i, place[0], 0, 0)),
            pl.BlockSpec((step, OWN, LANE), lambda i, place: (i, 0, 0)),
            pl.BlockSpec((PACK, KEYS), lambda i, place: (0, 0)),
            pl.BlockSpec((PACK, KEYS), lambda i, place: (0, 0)),
        ],
        pl.BlockSpec((step, OWN, KEYS), lambda i, place: (i, 0, 0)),
        jax.ShapeDtypeStruct((N_T // 2, OWN, KEYS), BF),
        2 * TOK // 2 * 2 * LANE * KEYS,
        7 * 1024 * 1024,
        [pltpu.VMEM((2 * LANE, KEYS), BF)],
    )(place, fresh, rows_other, packed_mine, packed_other)


def shards(upstream, stashed, returning, key_cotangent, key_weight, norm_gain, lengths):
    lane = lax.axis_index("ts")
    core = lane % 2
    half = (lane // 2) % 2
    z = lane // 4
    place = core.astype(jnp.int32)[None]
    gain = norm_gain[0]
    weights = key_weight[0]
    fresh = upstream[0]
    saved = stashed[0]

    def by_core(value):
        parts = value.reshape(N_T // 2, 2, OWN, *value.shape[1:])
        return [
            lax.dynamic_index_in_dim(parts, index, 1, keepdims=False).reshape(
                TOK // 2, *value.shape[1:]
            )
            for index in (core, 1 - core)
        ]

    packed = pack(place, weights, norm_gain)
    packed, fresh_rows = lax.optimization_barrier((packed, fresh))
    packed = move(packed, to_previous)

    cot_own = key_cotangent[0]
    cot_half = move(cot_own, to_other_half)
    cot_pair = jnp.stack(
        [jnp.where(half == 0, cot_own, cot_half), jnp.where(half == 0, cot_half, cot_own)]
    )
    lanes = [[q * 4 + j for q in range(N_Z)] for j in range(4)]
    cot_mine = lax.all_gather(cot_pair, "ts", axis=0, axis_index_groups=lanes, tiled=True)
    cot_mine = cot_mine.reshape(TOK // 2, KEYS)

    older_first = move(after(saved[:CUT], cot_half), to_mirror)

    rows = fresh.reshape(N_T // 2, 2, OWN, LANE)
    rows_other = fresh_rows.reshape(N_T // 2, 2, OWN, LANE)
    rows_other = move(
        lax.dynamic_index_in_dim(rows_other, 1 - core, 1, keepdims=False), to_other_core
    )

    packed_other = move(packed, to_other_core)
    partial = forward(place, rows, rows_other, packed, packed_other)

    def block(distance):
        return lax.dynamic_slice_in_dim(partial, ((z + distance) % N_Z) * 2, 2, 0)

    older_second = move(after(saved[CUT:], partial), to_mirror)

    fresh_wide = fresh.astype(F32)
    saved_wide = saved.astype(F32)
    fresh_part = jnp.sum(fresh_wide * fresh_wide, axis=1).reshape(N_Z, 2, 2, OWN)
    saved_part = jnp.sum(saved_wide * saved_wide, axis=1).reshape(1, N_T, OWN)
    squares = jnp.concatenate(
        [
            fresh_part.transpose(0, 2, 1, 3).reshape(N_T // 2, 2, OWN).astype(BF),
            jnp.broadcast_to(saved_part.astype(BF), (N_T // 2, N_T, OWN)),
        ],
        axis=1,
    )
    halves = [[q * 4 + h * 2 + c for q in range(N_Z) for c in range(2)] for h in range(2)]
    squares = lax.all_to_all(
        after(squares, older_first), "ts", 0, 0, axis_index_groups=halves, tiled=True
    )
    squares_raw = squares
    squares = jnp.sum(squares.astype(F32), axis=0)
    older_sq = [move(squares[2:], to_mirror), move(squares[2:], to_mirror_other_half)]
    fresh_other = move(after(squares[:2], *older_sq), to_other_half)

    downstream = move(after(returning[0], *older_sq), to_previous)

    up = move(block(4), z_up, (0,))
    down = move(block(4), z_down, (1,))
    up, down = lax.optimization_barrier((up, down, older_first, squares_raw))[:2]
    up = add(block(3), up)
    down = add(block(-3), down)
    up = move(up, z_up)
    down = move(down, z_down)
    up, down, cot_mine = lax.optimization_barrier(
        (up, down, cot_mine, older_second, *older_sq)
    )[:3]

    cots = [cot_mine, move(cot_mine, to_other_core)]
    raw = [
        lax.dot_general(cot, weights, (((1,), (1,)), ((), ())), preferred_element_type=F32)
        for cot in cots
    ]
    up = add(block(2), up)
    down = add(block(-2), down)
    older_first, older_second, *older_sq = lax.optimization_barrier(
        (older_first, older_second, *older_sq, up, down)
    )[:4]
    up = move(up, z_up)
    down = move(down, z_down)
    up, down, raw[0], fresh_other = lax.optimization_barrier((up, down, raw[0], fresh_other))
    up = add(block(1), up)
    down = add(block(-1), down)
    up = move(up, z_up)
    down = move(down, z_down)
    older = jnp.concatenate([older_first, older_second], axis=0)
    older_rate = lax.rsqrt((older_sq[0] + older_sq[1]) / WIDTH + eps).reshape(TOK)
    live = (jnp.arange(TOK, dtype=jnp.int32) < lengths[0]).astype(F32)
    scales = by_core(live * older_rate)
    grads = []
    curves = []
    lefts = []
    gain_grad = jnp.zeros((LANE,), F32)
    for cot, product, rows, scale in zip(cots, raw, by_core(older), scales):
        wide = rows.astype(F32)
        grad = scale[:, None] * product
        grads.append(grad)
        curves.append(jnp.sum(grad * (wide * gain).astype(BF).astype(F32), axis=1))
        gain_grad = gain_grad + jnp.sum(grad * wide, axis=0)
        lefts.append(wide * gain * scale[:, None])

    mine = (jnp.arange(2) == core)[None, :, None]
    curve = [part.reshape(N_T // 2, 1, OWN) for part in curves]
    curve = jnp.where(mine, curve[0], curve[1])
    curve = jnp.broadcast_to(curve.reshape(1, N_T, OWN).astype(BF), (N_T, N_T, OWN))
    curve = lax.all_to_all(curve, "ts", 0, 0, tiled=True)
    up, down = lax.optimization_barrier((up, down, curve, downstream))[:2]
    fresh_rate = lax.rsqrt((squares[:2] + fresh_other) / WIDTH + eps)
    curve = jnp.sum(curve.astype(F32), axis=0).reshape(TOK)
    pull = older_rate * older_rate / WIDTH * curve

    summed = block(0).astype(F32) + up.astype(F32) + down.astype(F32)
    straight = (pick(summed, half) * pick(fresh_rate, half)[:, None]).astype(BF)
    crossed = (pick(summed, 1 - half) * pick(fresh_rate, 1 - half)[:, None]).astype(BF)
    *cots, pull = lax.optimization_barrier((*cots, pull, straight, crossed))[:3]
    straight = move(straight, to_next)
    crossed = move(crossed, to_next_other_half)
    new_keys = (straight.astype(F32) + crossed.astype(F32)).astype(BF)

    weight_total = sum(
        lax.dot_general(
            left.astype(BF), cot, (((0,), (0,)), ((), ())), preferred_element_type=F32
        )
        for left, cot in zip(lefts, cots)
    )
    base = jnp.zeros((N_T // 2, 2, OWN, LANE), F32)
    for index, grad in zip((core, 1 - core), grads):
        base = lax.dynamic_update_index_in_dim(
            base, (gain * grad).reshape(N_T // 2, OWN, LANE), index, 1
        )
    base = base.reshape(TOK, LANE)
    total = downstream.astype(F32) + base - pull[:, None] * older.astype(F32)
    return (
        new_keys[None],
        total.astype(BF)[None],
        weight_total[None],
        gain_grad[None],
    )


def solution(mesh):
    return jax.shard_map(
        shards,
        mesh=mesh,
        in_specs=(
            P("section", None, "ts"),
            P("section", None, "ts"),
            P("section", None, "ts"),
            P("section", "ts", None),
            P("section", "ts", None),
            P("section", "ts"),
            P("section"),
        ),
        out_specs=(
            P("section", "ts", None),
            P("section", None, "ts"),
            P("section", "ts", None),
            P("section", "ts"),
        ),
        check_vma=False,
    )
```

```python
import jax
import jax.numpy as jnp
from jax import lax
from jax.experimental import pallas as pl
from jax.experimental.pallas import tpu as pltpu
from jax.sharding import PartitionSpec as P

eps = 1e-05
BF = jnp.bfloat16
F32 = jnp.float32
N_S = 8
N_T = 32
N_Z = 8
TOK = 4096
OWN = TOK // N_T
WIDTH = 8192
LANE = WIDTH // N_T
KEYS = 1024
PACK = LANE + 16
CUT = 3 * TOK // 4
SPLIT = TOK // 4
ORDER = 4
AXES = ("section", "ts")


def move(value, target, cores=(0, 1)):
    pairs = []
    for s in range(N_S):
        for t in [t for t in range(N_T) if t % 2 in cores]:
            to_s, to_t = target(s, t)
            pairs.append((s * N_T + t, to_s * N_T + to_t))
    return lax.ppermute(value, AXES, pairs)


def to_next(s, t):
    return (s + 1) % N_S, t


def to_previous(s, t):
    return (s - 1) % N_S, t


def to_mirror(s, t):
    return N_S - 1 - s, t


def to_mirror_other_half(s, t):
    return N_S - 1 - s, t ^ 2


def to_other_core(s, t):
    return s, t ^ 1


def to_other_half(s, t):
    return s, t ^ 2


def to_next_other_half(s, t):
    return (s + 1) % N_S, t ^ 2


def z_up(s, t):
    return s, (t + 4) % N_T


def z_down(s, t):
    return s, (t - 4) % N_T


def pick(value, index):
    return lax.dynamic_index_in_dim(value, index, 0, keepdims=False)


def after(value, *others):
    return lax.optimization_barrier((value,) + others)[0]


def add(a, b):
    return (a.astype(F32) + b.astype(F32)).astype(BF)


def call(kernel, grid, in_specs, out_specs, out_shape, flops, size, scratch=()):
    return pl.pallas_call(
        kernel,
        grid_spec=pltpu.PrefetchScalarGridSpec(
            num_scalar_prefetch=1,
            grid=grid,
            in_specs=in_specs,
            out_specs=out_specs,
            scratch_shapes=scratch,
        ),
        out_shape=out_shape,
        compiler_params=pltpu.CompilerParams(vmem_limit_bytes=24 * 1024 * 1024),
        cost_estimate=pl.CostEstimate(flops=flops, bytes_accessed=size, transcendentals=0),
    )


def pack_kernel(place, weights, gain, out):
    out[:LANE, :] = weights[...]
    value = gain[...]
    high = value.astype(BF)
    middle = (value - high.astype(F32)).astype(BF)
    low = (value - high.astype(F32) - middle.astype(F32)).astype(BF)
    row = jnp.concatenate([high, middle, low, jnp.zeros((1, LANE), BF)], axis=1)
    out[LANE:, :] = jnp.broadcast_to(row, (PACK - LANE, KEYS))


def pack(place, weights, gain):
    return call(
        pack_kernel,
        (1,),
        [
            pl.BlockSpec((LANE, KEYS), lambda i, place: (0, 0)),
            pl.BlockSpec((1, LANE), lambda i, place: (0, 0)),
        ],
        pl.BlockSpec((PACK, KEYS), lambda i, place: (0, 0)),
        jax.ShapeDtypeStruct((PACK, KEYS), BF),
        0,
        2 * PACK * KEYS * 2,
    )(place, weights, gain)


def forward_kernel(place, rows_mine, rows_other, packed_mine, packed_other, out, weights):
    rows = out.shape[0] * OWN

    @pl.when(pl.program_id(0) == 0)
    def _():
        weights[:LANE, :] = packed_mine[:LANE, :]
        weights[LANE:, :] = packed_other[:LANE, :]

    left = []
    for block, packed in ((rows_mine, packed_mine), (rows_other, packed_other)):
        pieces = packed[LANE : LANE + 1, :].astype(F32)
        gains = pieces[:, :LANE] + pieces[:, LANE : 2 * LANE] + pieces[:, 2 * LANE : 3 * LANE]
        left.append((block[...].reshape(rows, LANE).astype(F32) * gains).astype(BF))
    total = jnp.dot(jnp.concatenate(left, axis=1), weights[...], preferred_element_type=F32)
    out[...] = total.astype(BF).reshape(out.shape)


def forward(place, fresh, rows_other, packed_mine, packed_other):
    step = 4
    return call(
        forward_kernel,
        (N_T // 2 // step,),
        [
            pl.BlockSpec((step, 1, OWN, LANE), lambda i, place: (i, place[0], 0, 0)),
            pl.BlockSpec((step, OWN, LANE), lambda i, place: (i, 0, 0)),
            pl.BlockSpec((PACK, KEYS), lambda i, place: (0, 0)),
            pl.BlockSpec((PACK, KEYS), lambda i, place: (0, 0)),
        ],
        pl.BlockSpec((step, OWN, KEYS), lambda i, place: (i, 0, 0)),
        jax.ShapeDtypeStruct((N_T // 2, OWN, KEYS), BF),
        2 * TOK // 2 * 2 * LANE * KEYS,
        7 * 1024 * 1024,
        [pltpu.VMEM((2 * LANE, KEYS), BF)],
    )(place, fresh, rows_other, packed_mine, packed_other)


def order_kernel(place, mine, other, out):
    first = place[0] == 0
    out[:, 0] = jnp.where(first, mine[...], other[...])
    out[:, 1] = jnp.where(first, other[...], mine[...])


def order(place, mine, other):
    half = pl.BlockSpec((ORDER, OWN, LANE), lambda i, place: (i, 0, 0))
    return call(
        order_kernel,
        (N_T // 2 // ORDER,),
        [half, half],
        pl.BlockSpec((ORDER, 2, OWN, LANE), lambda i, place: (i, 0, 0, 0)),
        jax.ShapeDtypeStruct((N_T // 2, 2, OWN, LANE), F32),
        200 * TOK * LANE * KEYS,
        8 * TOK * LANE,
    )(place, mine, other)


def shards(upstream, stashed, returning, key_cotangent, key_weight, norm_gain, lengths):
    lane = lax.axis_index("ts")
    core = lane % 2
    half = (lane // 2) % 2
    z = lane // 4
    place = core.astype(jnp.int32)[None]
    gain = norm_gain[0]
    weights = key_weight[0]
    fresh = upstream[0]
    saved = stashed[0]

    def by_core(value):
        parts = value.reshape(N_T // 2, 2, OWN, *value.shape[1:])
        return [
            lax.dynamic_index_in_dim(parts, index, 1, keepdims=False).reshape(
                TOK // 2, *value.shape[1:]
            )
            for index in (core, 1 - core)
        ]

    packed = pack(place, weights, norm_gain)
    packed, fresh_rows = lax.optimization_barrier((packed, fresh))
    packed = move(packed, to_previous)

    cot_own = key_cotangent[0]
    cot_half = move(cot_own, to_other_half)
    cot_pair = jnp.stack(
        [jnp.where(half == 0, cot_own, cot_half), jnp.where(half == 0, cot_half, cot_own)]
    )
    lanes = [[q * 4 + j for q in range(N_Z)] for j in range(4)]
    cot_mine = lax.all_gather(cot_pair, "ts", axis=0, axis_index_groups=lanes, tiled=True)
    cot_mine = cot_mine.reshape(TOK // 2, KEYS)

    older_first = move(after(saved[:CUT], cot_half), to_mirror)

    rows = fresh.reshape(N_T // 2, 2, OWN, LANE)
    rows_other = fresh_rows.reshape(N_T // 2, 2, OWN, LANE)
    rows_other = move(
        lax.dynamic_index_in_dim(rows_other, 1 - core, 1, keepdims=False), to_other_core
    )

    fresh_wide = fresh.astype(F32)
    saved_wide = saved.astype(F32)
    fresh_part = jnp.sum(fresh_wide * fresh_wide, axis=1).reshape(N_Z, 2, 2, OWN)
    saved_part = jnp.sum(saved_wide * saved_wide, axis=1).reshape(1, N_T, OWN)
    squares = jnp.concatenate(
        [
            fresh_part.transpose(0, 2, 1, 3).reshape(N_T // 2, 2, OWN).astype(BF),
            jnp.broadcast_to(saved_part.astype(BF), (N_T // 2, N_T, OWN)),
        ],
        axis=1,
    )
    halves = [[q * 4 + h * 2 + c for q in range(N_Z) for c in range(2)] for h in range(2)]
    squares = lax.all_to_all(
        after(squares, packed), "ts", 0, 0, axis_index_groups=halves, tiled=True
    )
    squares_raw = squares
    squares = jnp.sum(squares.astype(F32), axis=0)
    older_sq = [move(squares[2:], to_mirror), move(squares[2:], to_mirror_other_half)]
    fresh_other = move(after(squares[:2], *older_sq), to_other_half)

    older_second = move(after(saved[CUT:], *older_sq), to_mirror)

    early = move(after(returning[0, :SPLIT], *older_sq), to_previous)
    late = returning[0, SPLIT:]

    packed_other = move(packed, to_other_core)
    partial = forward(place, rows, rows_other, packed, packed_other)

    def block(distance):
        return lax.dynamic_slice_in_dim(partial, ((z + distance) % N_Z) * 2, 2, 0)

    up = move(block(4), z_up, (0,))
    down = move(block(4), z_down, (1,))
    up, down, late, fresh_other = lax.optimization_barrier(
        (up, down, late, fresh_other, squares_raw, older_first, *older_sq)
    )[:4]
    up = add(block(3), up)
    down = add(block(-3), down)
    up = move(up, z_up)
    down = move(down, z_down)
    up, down, cot_mine = lax.optimization_barrier((up, down, cot_mine, older_second, early))[:3]

    cots = [cot_mine, move(cot_mine, to_other_core)]
    raw = [
        lax.dot_general(cot, weights, (((1,), (1,)), ((), ())), preferred_element_type=F32)
        for cot in cots
    ]
    up = add(block(2), up)
    down = add(block(-2), down)
    older_first, older_second, *older_sq = lax.optimization_barrier(
        (older_first, older_second, *older_sq, up, down)
    )[:4]
    late = move(after(late, up, down), to_previous)
    up = move(up, z_up)
    down = move(down, z_down)
    up, down, raw[0] = lax.optimization_barrier((up, down, raw[0]))
    up = add(block(1), up)
    down = add(block(-1), down)
    cots[1] = after(cots[1], up, down)
    raw[1] = lax.dot_general(
        cots[1], weights, (((1,), (1,)), ((), ())), preferred_element_type=F32
    )
    up = move(up, z_up)
    down = move(down, z_down)
    older = jnp.concatenate([older_first, older_second], axis=0)
    older_rate = lax.rsqrt((older_sq[0] + older_sq[1]) / WIDTH + eps).reshape(TOK)
    live = (jnp.arange(TOK, dtype=jnp.int32) < lengths[0]).astype(F32)
    scales = by_core(live * older_rate)
    grads = []
    curves = []
    lefts = []
    gain_grad = jnp.zeros((LANE,), F32)
    for cot, product, rows, scale in zip(cots, raw, by_core(older), scales):
        wide = rows.astype(F32)
        grad = scale[:, None] * product
        grads.append(grad)
        curves.append(jnp.sum(grad * (wide * gain).astype(BF).astype(F32), axis=1))
        gain_grad = gain_grad + jnp.sum(grad * wide, axis=0)
        lefts.append(wide * gain * scale[:, None])

    mine = (jnp.arange(2) == core)[None, :, None]
    curve = [part.reshape(N_T // 2, 1, OWN) for part in curves]
    curve = jnp.where(mine, curve[0], curve[1])
    curve = jnp.broadcast_to(curve.reshape(1, N_T, OWN).astype(BF), (N_T, N_T, OWN))
    base = order(
        place, *[(gain * grad).reshape(N_T // 2, OWN, LANE) for grad in grads]
    ).reshape(TOK, LANE)
    curve = lax.all_to_all(curve, "ts", 0, 0, tiled=True)
    curve, base = lax.optimization_barrier((curve, base))
    up, down = lax.optimization_barrier((up, down, curve, late))[:2]
    fresh_rate = lax.rsqrt((squares[:2] + fresh_other) / WIDTH + eps)
    curve = jnp.sum(curve.astype(F32), axis=0).reshape(TOK)
    pull = older_rate * older_rate / WIDTH * curve

    summed = block(0).astype(F32) + up.astype(F32) + down.astype(F32)
    straight = (pick(summed, half) * pick(fresh_rate, half)[:, None]).astype(BF)
    crossed = (pick(summed, 1 - half) * pick(fresh_rate, 1 - half)[:, None]).astype(BF)
    *cots, pull = lax.optimization_barrier((*cots, pull, straight, crossed))[:3]
    straight = move(straight, to_next)
    crossed = move(crossed, to_next_other_half)
    new_keys = (straight.astype(F32) + crossed.astype(F32)).astype(BF)

    weight_total = sum(
        lax.dot_general(
            left.astype(BF), cot, (((0,), (0,)), ((), ())), preferred_element_type=F32
        )
        for left, cot in zip(lefts, cots)
    )
    downstream = jnp.concatenate([early, late], axis=0)
    total = downstream.astype(F32) + base - pull[:, None] * older.astype(F32)
    return (
        new_keys[None],
        total.astype(BF)[None],
        weight_total[None],
        gain_grad[None],
    )


def solution(mesh):
    return jax.shard_map(
        shards,
        mesh=mesh,
        in_specs=(
            P("section", None, "ts"),
            P("section", None, "ts"),
            P("section", None, "ts"),
            P("section", "ts", None),
            P("section", "ts", None),
            P("section", "ts"),
            P("section"),
        ),
        out_specs=(
            P("section", "ts", None),
            P("section", None, "ts"),
            P("section", "ts", None),
            P("section", "ts"),
        ),
        check_vma=False,
    )
```

```python
import jax
import jax.numpy as jnp
from jax import lax
from jax.experimental import pallas as pl
from jax.experimental.pallas import tpu as pltpu
from jax.sharding import PartitionSpec as P

eps = 1e-05
BF = jnp.bfloat16
F32 = jnp.float32
N_S = 8
N_T = 32
N_Z = 8
TOK = 4096
OWN = TOK // N_T
WIDTH = 8192
LANE = WIDTH // N_T
KEYS = 1024
PACK = LANE + 16
CUT = 3 * TOK // 4
SPLIT = TOK // 4
ORDER = 4
AXES = ("section", "ts")


def move(value, target, cores=(0, 1)):
    pairs = []
    for s in range(N_S):
        for t in [t for t in range(N_T) if t % 2 in cores]:
            to_s, to_t = target(s, t)
            pairs.append((s * N_T + t, to_s * N_T + to_t))
    return lax.ppermute(value, AXES, pairs)


def to_next(s, t):
    return (s + 1) % N_S, t


def to_previous(s, t):
    return (s - 1) % N_S, t


def to_mirror(s, t):
    return N_S - 1 - s, t


def to_mirror_other_half(s, t):
    return N_S - 1 - s, t ^ 2


def to_other_core(s, t):
    return s, t ^ 1


def to_other_half(s, t):
    return s, t ^ 2


def to_next_other_half(s, t):
    return (s + 1) % N_S, t ^ 2


def z_up(s, t):
    return s, (t + 4) % N_T


def z_down(s, t):
    return s, (t - 4) % N_T


def pick(value, index):
    return lax.dynamic_index_in_dim(value, index, 0, keepdims=False)


def after(value, *others):
    return lax.optimization_barrier((value,) + others)[0]


def add(a, b):
    return (a.astype(F32) + b.astype(F32)).astype(BF)


def call(kernel, grid, in_specs, out_specs, out_shape, flops, size, scratch=()):
    return pl.pallas_call(
        kernel,
        grid_spec=pltpu.PrefetchScalarGridSpec(
            num_scalar_prefetch=1,
            grid=grid,
            in_specs=in_specs,
            out_specs=out_specs,
            scratch_shapes=scratch,
        ),
        out_shape=out_shape,
        compiler_params=pltpu.CompilerParams(vmem_limit_bytes=24 * 1024 * 1024),
        cost_estimate=pl.CostEstimate(flops=flops, bytes_accessed=size, transcendentals=0),
    )


def pack_kernel(place, weights, gain, out):
    out[:LANE, :] = weights[...]
    value = gain[...]
    high = value.astype(BF)
    middle = (value - high.astype(F32)).astype(BF)
    low = (value - high.astype(F32) - middle.astype(F32)).astype(BF)
    row = jnp.concatenate([high, middle, low, jnp.zeros((1, LANE), BF)], axis=1)
    out[LANE:, :] = jnp.broadcast_to(row, (PACK - LANE, KEYS))


def pack(place, weights, gain):
    return call(
        pack_kernel,
        (1,),
        [
            pl.BlockSpec((LANE, KEYS), lambda i, place: (0, 0)),
            pl.BlockSpec((1, LANE), lambda i, place: (0, 0)),
        ],
        pl.BlockSpec((PACK, KEYS), lambda i, place: (0, 0)),
        jax.ShapeDtypeStruct((PACK, KEYS), BF),
        0,
        2 * PACK * KEYS * 2,
    )(place, weights, gain)


def forward_kernel(place, rows_mine, rows_other, packed_mine, packed_other, out, weights):
    rows = out.shape[0] * OWN

    @pl.when(pl.program_id(0) == 0)
    def _():
        weights[:LANE, :] = packed_mine[:LANE, :]
        weights[LANE:, :] = packed_other[:LANE, :]

    left = []
    for block, packed in ((rows_mine, packed_mine), (rows_other, packed_other)):
        pieces = packed[LANE : LANE + 1, :].astype(F32)
        gains = pieces[:, :LANE] + pieces[:, LANE : 2 * LANE] + pieces[:, 2 * LANE : 3 * LANE]
        left.append((block[...].reshape(rows, LANE).astype(F32) * gains).astype(BF))
    total = jnp.dot(jnp.concatenate(left, axis=1), weights[...], preferred_element_type=F32)
    out[...] = total.astype(BF).reshape(out.shape)


def forward(place, fresh, rows_other, packed_mine, packed_other):
    step = 4
    return call(
        forward_kernel,
        (N_T // 2 // step,),
        [
            pl.BlockSpec((step, 1, OWN, LANE), lambda i, place: (i, place[0], 0, 0)),
            pl.BlockSpec((step, OWN, LANE), lambda i, place: (i, 0, 0)),
            pl.BlockSpec((PACK, KEYS), lambda i, place: (0, 0)),
            pl.BlockSpec((PACK, KEYS), lambda i, place: (0, 0)),
        ],
        pl.BlockSpec((step, OWN, KEYS), lambda i, place: (i, 0, 0)),
        jax.ShapeDtypeStruct((N_T // 2, OWN, KEYS), BF),
        2 * TOK // 2 * 2 * LANE * KEYS,
        7 * 1024 * 1024,
        [pltpu.VMEM((2 * LANE, KEYS), BF)],
    )(place, fresh, rows_other, packed_mine, packed_other)


def order_kernel(place, mine, other, out):
    first = place[0] == 0
    out[:, 0] = jnp.where(first, mine[...], other[...])
    out[:, 1] = jnp.where(first, other[...], mine[...])


def order(place, mine, other):
    half = pl.BlockSpec((ORDER, OWN, LANE), lambda i, place: (i, 0, 0))
    return call(
        order_kernel,
        (N_T // 2 // ORDER,),
        [half, half],
        pl.BlockSpec((ORDER, 2, OWN, LANE), lambda i, place: (i, 0, 0, 0)),
        jax.ShapeDtypeStruct((N_T // 2, 2, OWN, LANE), F32),
        200 * TOK * LANE * KEYS,
        8 * TOK * LANE,
    )(place, mine, other)


def shards(upstream, stashed, returning, key_cotangent, key_weight, norm_gain, lengths):
    lane = lax.axis_index("ts")
    core = lane % 2
    half = (lane // 2) % 2
    z = lane // 4
    place = core.astype(jnp.int32)[None]
    gain = norm_gain[0]
    weights = key_weight[0]
    fresh = upstream[0]
    saved = stashed[0]

    def by_core(value):
        parts = value.reshape(N_T // 2, 2, OWN, *value.shape[1:])
        return [
            lax.dynamic_index_in_dim(parts, index, 1, keepdims=False).reshape(
                TOK // 2, *value.shape[1:]
            )
            for index in (core, 1 - core)
        ]

    packed = pack(place, weights, norm_gain)
    packed, fresh_rows = lax.optimization_barrier((packed, fresh))
    packed = move(packed, to_previous)

    cot_own = key_cotangent[0]
    cot_half = move(cot_own, to_other_half)
    cot_pair = jnp.stack(
        [jnp.where(half == 0, cot_own, cot_half), jnp.where(half == 0, cot_half, cot_own)]
    )
    lanes = [[q * 4 + j for q in range(N_Z)] for j in range(4)]
    cot_mine = lax.all_gather(cot_pair, "ts", axis=0, axis_index_groups=lanes, tiled=True)
    cot_mine = cot_mine.reshape(TOK // 2, KEYS)

    older_first = move(after(saved[:CUT], cot_half), to_mirror)

    rows = fresh.reshape(N_T // 2, 2, OWN, LANE)
    rows_other = fresh_rows.reshape(N_T // 2, 2, OWN, LANE)
    rows_other = move(
        lax.dynamic_index_in_dim(rows_other, 1 - core, 1, keepdims=False), to_other_core
    )

    fresh_wide = fresh.astype(F32)
    saved_wide = saved.astype(F32)
    fresh_part = jnp.sum(fresh_wide * fresh_wide, axis=1).reshape(N_Z, 2, 2, OWN)
    saved_part = jnp.sum(saved_wide * saved_wide, axis=1).reshape(1, N_T, OWN)
    squares = jnp.concatenate(
        [
            fresh_part.transpose(0, 2, 1, 3).reshape(N_T // 2, 2, OWN).astype(BF),
            jnp.broadcast_to(saved_part.astype(BF), (N_T // 2, N_T, OWN)),
        ],
        axis=1,
    )
    halves = [[q * 4 + h * 2 + c for q in range(N_Z) for c in range(2)] for h in range(2)]
    squares = lax.all_to_all(
        after(squares, packed), "ts", 0, 0, axis_index_groups=halves, tiled=True
    )
    squares_raw = squares
    squares = jnp.sum(squares.astype(F32), axis=0)
    older_sq = [move(squares[2:], to_mirror), move(squares[2:], to_mirror_other_half)]
    fresh_other = move(after(squares[:2], *older_sq), to_other_half)

    older_second = move(after(saved[CUT:], *older_sq), to_mirror)

    early = move(after(returning[0, :SPLIT], *older_sq), to_previous)
    late = returning[0, SPLIT:]

    packed_other = move(packed, to_other_core)
    partial = forward(place, rows, rows_other, packed, packed_other)

    def block(distance):
        return lax.dynamic_slice_in_dim(partial, ((z + distance) % N_Z) * 2, 2, 0)

    up = move(block(4), z_up, (0,))
    down = move(block(4), z_down, (1,))
    up, down, late, fresh_other = lax.optimization_barrier(
        (up, down, late, fresh_other, squares_raw, older_first, *older_sq)
    )[:4]
    up = add(block(3), up)
    down = add(block(-3), down)
    up = move(up, z_up)
    down = move(down, z_down)
    up, down, cot_mine = lax.optimization_barrier((up, down, cot_mine, older_second, early))[:3]

    cots = [cot_mine, move(cot_mine, to_other_core)]
    raw = [
        lax.dot_general(cot, weights, (((1,), (1,)), ((), ())), preferred_element_type=F32)
        for cot in cots
    ]
    up = add(block(2), up)
    down = add(block(-2), down)
    older_first, older_second, *older_sq = lax.optimization_barrier(
        (older_first, older_second, *older_sq, up, down)
    )[:4]
    late = move(after(late, up, down), to_previous)
    up = move(up, z_up)
    down = move(down, z_down)
    up, down, raw[0] = lax.optimization_barrier((up, down, raw[0]))
    up = add(block(1), up)
    down = add(block(-1), down)
    cots[1] = after(cots[1], up, down)
    raw[1] = lax.dot_general(
        cots[1], weights, (((1,), (1,)), ((), ())), preferred_element_type=F32
    )
    up = move(up, z_up)
    down = move(down, z_down)
    older = jnp.concatenate([older_first, older_second], axis=0)
    older_rate = lax.rsqrt((older_sq[0] + older_sq[1]) / WIDTH + eps).reshape(TOK)
    live = (jnp.arange(TOK, dtype=jnp.int32) < lengths[0]).astype(F32)
    scales = by_core(live * older_rate)
    grads = []
    curves = []
    lefts = []
    gain_grad = jnp.zeros((LANE,), F32)
    for cot, product, rows, scale in zip(cots, raw, by_core(older), scales):
        wide = rows.astype(F32)
        grad = scale[:, None] * product
        grads.append(grad)
        curves.append(jnp.sum(grad * (wide * gain).astype(BF).astype(F32), axis=1))
        gain_grad = gain_grad + jnp.sum(grad * wide, axis=0)
        lefts.append(wide * gain * scale[:, None])

    mine = (jnp.arange(2) == core)[None, :, None]
    curve = [part.reshape(N_T // 2, 1, OWN) for part in curves]
    curve = jnp.where(mine, curve[0], curve[1])
    curve = jnp.broadcast_to(curve.reshape(1, N_T, OWN).astype(BF), (N_T, N_T, OWN))
    base = order(
        place, *[(gain * grad).reshape(N_T // 2, OWN, LANE) for grad in grads]
    ).reshape(TOK, LANE)
    curve = lax.all_to_all(curve, "ts", 0, 0, tiled=True)
    up, down, base = lax.optimization_barrier((up, down, base, late))[:3]
    fresh_rate = lax.rsqrt((squares[:2] + fresh_other) / WIDTH + eps)

    summed = block(0).astype(F32) + up.astype(F32) + down.astype(F32)
    straight = (pick(summed, half) * pick(fresh_rate, half)[:, None]).astype(BF)
    crossed = (pick(summed, 1 - half) * pick(fresh_rate, 1 - half)[:, None]).astype(BF)
    *cots, curve = lax.optimization_barrier((*cots, curve, straight, crossed))[:3]
    curve = jnp.sum(curve.astype(F32), axis=0).reshape(TOK)
    pull = older_rate * older_rate / WIDTH * curve
    straight = move(straight, to_next)
    crossed = move(crossed, to_next_other_half)

    weight_total = sum(
        lax.dot_general(
            left.astype(BF), cot, (((0,), (0,)), ((), ())), preferred_element_type=F32
        )
        for left, cot in zip(lefts, cots)
    )
    downstream = jnp.concatenate([early, late], axis=0)
    total = downstream.astype(F32) + base - pull[:, None] * older.astype(F32)
    straight, crossed = lax.optimization_barrier((straight, crossed, weight_total, total))[:2]
    new_keys = (straight.astype(F32) + crossed.astype(F32)).astype(BF)
    return (
        new_keys[None],
        total.astype(BF)[None],
        weight_total[None],
        gain_grad[None],
    )


def solution(mesh):
    return jax.shard_map(
        shards,
        mesh=mesh,
        in_specs=(
            P("section", None, "ts"),
            P("section", None, "ts"),
            P("section", None, "ts"),
            P("section", "ts", None),
            P("section", "ts", None),
            P("section", "ts"),
            P("section"),
        ),
        out_specs=(
            P("section", "ts", None),
            P("section", None, "ts"),
            P("section", "ts", None),
            P("section", "ts"),
        ),
        check_vma=False,
    )
```

```python
import jax
import jax.numpy as jnp
from jax import lax
from jax.experimental import pallas as pl
from jax.experimental.pallas import tpu as pltpu
from jax.sharding import PartitionSpec as P

eps = 1e-05
BF = jnp.bfloat16
F32 = jnp.float32
N_S = 8
N_T = 32
N_Z = 8
TOK = 4096
OWN = TOK // N_T
WIDTH = 8192
LANE = WIDTH // N_T
KEYS = 1024
PACK = LANE + 16
CUT = 3 * TOK // 4
SPLIT = TOK // 4
ORDER = 4
AXES = ("section", "ts")


def move(value, target, cores=(0, 1)):
    pairs = []
    for s in range(N_S):
        for t in [t for t in range(N_T) if t % 2 in cores]:
            to_s, to_t = target(s, t)
            pairs.append((s * N_T + t, to_s * N_T + to_t))
    return lax.ppermute(value, AXES, pairs)


def to_next(s, t):
    return (s + 1) % N_S, t


def to_previous(s, t):
    return (s - 1) % N_S, t


def to_mirror(s, t):
    return N_S - 1 - s, t


def to_mirror_other_half(s, t):
    return N_S - 1 - s, t ^ 2


def to_other_core(s, t):
    return s, t ^ 1


def to_other_half(s, t):
    return s, t ^ 2


def to_next_other_half(s, t):
    return (s + 1) % N_S, t ^ 2


def z_up(s, t):
    return s, (t + 4) % N_T


def z_down(s, t):
    return s, (t - 4) % N_T


def pick(value, index):
    return lax.dynamic_index_in_dim(value, index, 0, keepdims=False)


def after(value, *others):
    return lax.optimization_barrier((value,) + others)[0]


def add(a, b):
    return (a.astype(F32) + b.astype(F32)).astype(BF)


def call(kernel, grid, in_specs, out_specs, out_shape, flops, size, scratch=()):
    return pl.pallas_call(
        kernel,
        grid_spec=pltpu.PrefetchScalarGridSpec(
            num_scalar_prefetch=1,
            grid=grid,
            in_specs=in_specs,
            out_specs=out_specs,
            scratch_shapes=scratch,
        ),
        out_shape=out_shape,
        compiler_params=pltpu.CompilerParams(vmem_limit_bytes=24 * 1024 * 1024),
        cost_estimate=pl.CostEstimate(flops=flops, bytes_accessed=size, transcendentals=0),
    )


def pack_kernel(place, weights, gain, out):
    out[:LANE, :] = weights[...]
    value = gain[...]
    high = value.astype(BF)
    middle = (value - high.astype(F32)).astype(BF)
    low = (value - high.astype(F32) - middle.astype(F32)).astype(BF)
    row = jnp.concatenate([high, middle, low, jnp.zeros((1, LANE), BF)], axis=1)
    out[LANE:, :] = jnp.broadcast_to(row, (PACK - LANE, KEYS))


def pack(place, weights, gain):
    return call(
        pack_kernel,
        (1,),
        [
            pl.BlockSpec((LANE, KEYS), lambda i, place: (0, 0)),
            pl.BlockSpec((1, LANE), lambda i, place: (0, 0)),
        ],
        pl.BlockSpec((PACK, KEYS), lambda i, place: (0, 0)),
        jax.ShapeDtypeStruct((PACK, KEYS), BF),
        0,
        2 * PACK * KEYS * 2,
    )(place, weights, gain)


def forward_kernel(place, rows_mine, rows_other, packed_mine, packed_other, out, weights):
    rows = out.shape[0] * OWN

    @pl.when(pl.program_id(0) == 0)
    def _():
        weights[:LANE, :] = packed_mine[:LANE, :]
        weights[LANE:, :] = packed_other[:LANE, :]

    left = []
    for block, packed in ((rows_mine, packed_mine), (rows_other, packed_other)):
        pieces = packed[LANE : LANE + 1, :].astype(F32)
        gains = pieces[:, :LANE] + pieces[:, LANE : 2 * LANE] + pieces[:, 2 * LANE : 3 * LANE]
        left.append((block[...].reshape(rows, LANE).astype(F32) * gains).astype(BF))
    total = jnp.dot(jnp.concatenate(left, axis=1), weights[...], preferred_element_type=F32)
    out[...] = total.astype(BF).reshape(out.shape)


def forward(place, fresh, rows_other, packed_mine, packed_other):
    step = 4
    return call(
        forward_kernel,
        (N_T // 2 // step,),
        [
            pl.BlockSpec((step, 1, OWN, LANE), lambda i, place: (i, place[0], 0, 0)),
            pl.BlockSpec((step, OWN, LANE), lambda i, place: (i, 0, 0)),
            pl.BlockSpec((PACK, KEYS), lambda i, place: (0, 0)),
            pl.BlockSpec((PACK, KEYS), lambda i, place: (0, 0)),
        ],
        pl.BlockSpec((step, OWN, KEYS), lambda i, place: (i, 0, 0)),
        jax.ShapeDtypeStruct((N_T // 2, OWN, KEYS), BF),
        2 * TOK // 2 * 2 * LANE * KEYS,
        7 * 1024 * 1024,
        [pltpu.VMEM((2 * LANE, KEYS), BF)],
    )(place, fresh, rows_other, packed_mine, packed_other)


def order_kernel(place, mine, other, out):
    first = place[0] == 0
    out[:, 0] = jnp.where(first, mine[...], other[...])
    out[:, 1] = jnp.where(first, other[...], mine[...])


def order(place, mine, other):
    half = pl.BlockSpec((ORDER, OWN, LANE), lambda i, place: (i, 0, 0))
    return call(
        order_kernel,
        (N_T // 2 // ORDER,),
        [half, half],
        pl.BlockSpec((ORDER, 2, OWN, LANE), lambda i, place: (i, 0, 0, 0)),
        jax.ShapeDtypeStruct((N_T // 2, 2, OWN, LANE), F32),
        200 * TOK * LANE * KEYS,
        8 * TOK * LANE,
    )(place, mine, other)


def shards(upstream, stashed, returning, key_cotangent, key_weight, norm_gain, lengths):
    lane = lax.axis_index("ts")
    core = lane % 2
    half = (lane // 2) % 2
    z = lane // 4
    place = core.astype(jnp.int32)[None]
    gain = norm_gain[0]
    weights = key_weight[0]
    fresh = upstream[0]
    saved = stashed[0]

    def by_core(value):
        parts = value.reshape(N_T // 2, 2, OWN, *value.shape[1:])
        return [
            lax.dynamic_index_in_dim(parts, index, 1, keepdims=False).reshape(
                TOK // 2, *value.shape[1:]
            )
            for index in (core, 1 - core)
        ]

    packed = pack(place, weights, norm_gain)
    packed, fresh_rows = lax.optimization_barrier((packed, fresh))
    packed = move(packed, to_previous)

    cot_own = key_cotangent[0]
    cot_half = move(cot_own, to_other_half)
    cot_pair = jnp.stack(
        [jnp.where(half == 0, cot_own, cot_half), jnp.where(half == 0, cot_half, cot_own)]
    )
    lanes = [[q * 4 + j for q in range(N_Z)] for j in range(4)]
    cot_mine = lax.all_gather(cot_pair, "ts", axis=0, axis_index_groups=lanes, tiled=True)
    cot_mine = cot_mine.reshape(TOK // 2, KEYS)

    older_first = move(after(saved[:CUT], cot_half), to_mirror)

    rows = fresh.reshape(N_T // 2, 2, OWN, LANE)
    rows_other = fresh_rows.reshape(N_T // 2, 2, OWN, LANE)
    rows_other = move(
        lax.dynamic_index_in_dim(rows_other, 1 - core, 1, keepdims=False), to_other_core
    )

    fresh_wide = fresh.astype(F32)
    saved_wide = saved.astype(F32)
    fresh_part = jnp.sum(fresh_wide * fresh_wide, axis=1).reshape(N_Z, 2, 2, OWN)
    saved_part = jnp.sum(saved_wide * saved_wide, axis=1).reshape(1, N_T, OWN)
    squares = jnp.concatenate(
        [
            fresh_part.transpose(0, 2, 1, 3).reshape(N_T // 2, 2, OWN).astype(BF),
            jnp.broadcast_to(saved_part.astype(BF), (N_T // 2, N_T, OWN)),
        ],
        axis=1,
    )
    halves = [[q * 4 + h * 2 + c for q in range(N_Z) for c in range(2)] for h in range(2)]
    squares = lax.all_to_all(
        after(squares, packed), "ts", 0, 0, axis_index_groups=halves, tiled=True
    )
    squares_raw = squares
    squares = jnp.sum(squares.astype(F32), axis=0)
    older_sq = [move(squares[2:], to_mirror), move(squares[2:], to_mirror_other_half)]
    fresh_other = move(after(squares[:2], *older_sq), to_other_half)

    older_second = move(after(saved[CUT:], *older_sq), to_mirror)

    early = move(after(returning[0, :SPLIT], *older_sq), to_previous)
    late = returning[0, SPLIT:]

    packed_other = move(packed, to_other_core)
    partial = forward(place, rows, rows_other, packed, packed_other)

    def block(distance):
        return lax.dynamic_slice_in_dim(partial, ((z + distance) % N_Z) * 2, 2, 0)

    up = move(block(4), z_up, (0,))
    down = move(block(4), z_down, (1,))
    up, down, late, fresh_other = lax.optimization_barrier(
        (up, down, late, fresh_other, squares_raw, older_first, *older_sq)
    )[:4]
    up = add(block(3), up)
    down = add(block(-3), down)
    up = move(up, z_up)
    down = move(down, z_down)
    up, down, cot_mine = lax.optimization_barrier((up, down, cot_mine, older_second, early))[:3]

    cots = [cot_mine, move(cot_mine, to_other_core)]
    raw = [
        lax.dot_general(cot, weights, (((1,), (1,)), ((), ())), preferred_element_type=F32)
        for cot in cots
    ]
    up = add(block(2), up)
    down = add(block(-2), down)
    older_first, older_second, *older_sq = lax.optimization_barrier(
        (older_first, older_second, *older_sq, up, down)
    )[:4]
    late = move(after(late, up, down), to_previous)
    up = move(up, z_up)
    down = move(down, z_down)
    up, down, raw[0] = lax.optimization_barrier((up, down, raw[0]))
    up = add(block(1), up)
    down = add(block(-1), down)
    cots[1] = after(cots[1], up, down)
    raw[1] = lax.dot_general(
        cots[1], weights, (((1,), (1,)), ((), ())), preferred_element_type=F32
    )
    up = move(up, z_up)
    down = move(down, z_down)
    older = jnp.concatenate([older_first, older_second], axis=0)
    older_rate = lax.rsqrt((older_sq[0] + older_sq[1]) / WIDTH + eps).reshape(TOK)
    live = (jnp.arange(TOK, dtype=jnp.int32) < lengths[0]).astype(F32)
    scales = by_core(live * older_rate)
    grads = []
    curves = []
    lefts = []
    gain_grad = jnp.zeros((LANE,), F32)
    for cot, product, rows, scale in zip(cots, raw, by_core(older), scales):
        wide = rows.astype(F32)
        grad = scale[:, None] * product
        grads.append(grad)
        curves.append(jnp.sum(grad * (wide * gain).astype(BF).astype(F32), axis=1))
        gain_grad = gain_grad + jnp.sum(grad * wide, axis=0)
        lefts.append(wide * gain * scale[:, None])

    mine = (jnp.arange(2) == core)[None, :, None]
    curve = [part.reshape(N_T // 2, 1, OWN) for part in curves]
    curve = jnp.where(mine, curve[0], curve[1])
    curve = jnp.broadcast_to(curve.reshape(1, N_T, OWN).astype(BF), (N_T, N_T, OWN))
    base = order(
        place, *[(gain * grad).reshape(N_T // 2, OWN, LANE) for grad in grads]
    ).reshape(TOK, LANE)
    curve = lax.all_to_all(curve, "ts", 0, 0, tiled=True)
    up, down, base = lax.optimization_barrier((up, down, base))
    fresh_rate = lax.rsqrt((squares[:2] + fresh_other) / WIDTH + eps)

    summed = block(0).astype(F32) + up.astype(F32) + down.astype(F32)
    straight = (pick(summed, half) * pick(fresh_rate, half)[:, None]).astype(BF)
    crossed = (pick(summed, 1 - half) * pick(fresh_rate, 1 - half)[:, None]).astype(BF)
    *cots, curve = lax.optimization_barrier((*cots, curve, straight, crossed))[:3]
    curve = jnp.sum(curve.astype(F32), axis=0).reshape(TOK)
    pull = older_rate * older_rate / WIDTH * curve
    straight = move(straight, to_next)
    crossed = move(crossed, to_next_other_half)

    weight_total = sum(
        lax.dot_general(
            left.astype(BF), cot, (((0,), (0,)), ((), ())), preferred_element_type=F32
        )
        for left, cot in zip(lefts, cots)
    )
    downstream = jnp.concatenate([early, late], axis=0)
    total = downstream.astype(F32) + base - pull[:, None] * older.astype(F32)
    straight, crossed = lax.optimization_barrier((straight, crossed, weight_total, total))[:2]
    new_keys = (straight.astype(F32) + crossed.astype(F32)).astype(BF)
    return (
        new_keys[None],
        total.astype(BF)[None],
        weight_total[None],
        gain_grad[None],
    )


def solution(mesh):
    return jax.shard_map(
        shards,
        mesh=mesh,
        in_specs=(
            P("section", None, "ts"),
            P("section", None, "ts"),
            P("section", None, "ts"),
            P("section", "ts", None),
            P("section", "ts", None),
            P("section", "ts"),
            P("section"),
        ),
        out_specs=(
            P("section", "ts", None),
            P("section", None, "ts"),
            P("section", "ts", None),
            P("section", "ts"),
        ),
        check_vma=False,
    )
```
